256 devices in a mesh: dp: 8 (over y, core), seq: 32 (over x, z).
Axes of the slice: x: 4, y: 4, z: 8, core: 2. Of those that a mesh axis runs over, the one named last changes fastest.
Arguments:
- xbc: bfloat16 [131072, 4352], P(('dp', 'seq')), parts along dimension 0, may hold values from -6 to 6
- dt_raw: bfloat16 [131072, 64], P(('dp', 'seq')), parts along dimension 0, may hold values from -2.3 to 2.3
- conv_weight: float32 [4, 4352], replicated, may hold values from -3 to 3
- conv_bias: float32 [4352], replicated, may hold values from -1.5 to 1.5
- dt_bias: float32 [64], replicated, may hold values from -4 to -2
- a_log: float32 [64], replicated, may hold values from -8.6 to -0.2
- d_skip: float32 [64], replicated, may hold values from 0.5 to 2
- doc_lengths: int32 [128], P('dp'), parts along dimension 0, may hold values from 1 to 4096, 16384 in all
- loader_dest: int32 [1024], P('dp'), parts along dimension 0, may hold values from 0 to 127, as said below
Outputs:
- layer_out: bfloat16 [131072, 4096], P(('dp', 'seq')), parts along dimension 0
The draws below stay inside these ranges and needn't reach their ends.
There are 8 independent parts, one for each index of `dp`. The reference program is written for one: setup_inputs(seed, part) draws one part's arguments, and reference() takes and returns one part's arrays. A program takes and returns all parts, laid end to end along the dimension named above; an argument that names none is the same for every part. Nothing has to cross between parts.
Inputs may be any that keep to these rules, and one draw needn't show every extreme that they name: `loader_dest`: a permutation of the block numbers; the loader block at index b lies on seq device b // 4 and goes to a sequence block on a device at most 2 steps away along seq, counted around the axis; every device sends blocks to exactly four of the five devices within that reach (itself among the five), and exactly 1 block to each of the four. `doc_lengths`: they sum to 16384.
All inputs are finite; a program needn't handle non-finite values.
Results may differ from the reference program's by a relative error of at most 0.006.
Values may be sent and summed in bfloat16 or wider, within the bound.
A program may use at most 256 MiB of HBM per device.

```python
import math
import jax
import jax.numpy as jnp
import numpy as np
from jax import lax

H = 64
P_SIZE = 64
NS = 128
GROUP = 256
KW = 4
BLOCK_ROWS = 128
TOK_DEV = 512
TOKENS = 16384
BLOCKS = 128
DOCS = 16
WIDTH = 4352


def draw_a_log(key, part):
    key = jax.random.fold_in(key, 5)
    keys = jax.random.split(key, 3)
    share = 0.5
    pick = jax.random.uniform(keys[0], (H,))
    fast = jax.random.uniform(keys[1], (H,), minval=math.log(0.3), maxval=math.log(0.8))
    slow = jax.random.uniform(keys[2], (H,), minval=math.log(0.0002), maxval=math.log(0.002))
    return jnp.where(pick < share, fast, slow).astype(jnp.float32)


def draw_dt_raw(key, part):
    key = jax.random.fold_in(key, 7)
    keys = jax.random.split(key, 2)
    offset = jax.random.uniform(keys[0], (BLOCKS, 1, H), minval=-0.8, maxval=0.8)
    noise = jnp.clip(0.5 * jax.random.normal(keys[1], (BLOCKS, BLOCK_ROWS, H)), -1.5, 1.5)
    return (offset + noise).reshape(TOKENS, H).astype(jnp.bfloat16)


def ranked(key, valid, entries):
    rows = valid.shape[0]
    scores = jax.vmap(lambda k: jax.random.permutation(k, entries))(jax.random.split(key, rows))
    scores = scores.astype(jnp.int32) + (1 - valid.astype(jnp.int32)) * entries
    return jnp.argsort(jnp.argsort(scores, axis=1, stable=True), axis=1, stable=True).astype(jnp.int32)


def draw_loader_dest(key, part):
    key = jax.random.fold_in(key, 13)
    per_dev = TOK_DEV // BLOCK_ROWS
    count = BLOCKS // per_dev
    per_pair = per_dev // 4
    entries = 5 * per_pair
    keys = jax.random.split(key, 4)
    devices = jnp.arange(count, dtype=jnp.int32)
    flip_one = jax.random.randint(keys[0], (count // 2,), 0, 2)
    flip_two = jax.random.randint(keys[1], (count // 2,), 0, 2)
    first = jnp.where(jnp.repeat(flip_one, 2) == 1, devices ^ 1, devices)
    odd = devices % 2 == 1
    partner = jnp.where(odd, (devices + 1) % count, (devices - 1) % count)
    pair_two = jnp.where(odd, devices // 2, (devices - 1) % count // 2)
    second = jnp.where(flip_two[pair_two] == 1, partner, devices)
    skipped = second[first]
    offsets = jnp.repeat(jnp.arange(5, dtype=jnp.int32) - 2, per_pair)
    target = (devices[:, None] + offsets[None, :]) % count
    valid_out = target != skipped[:, None]
    source = (devices[:, None] - offsets[None, :]) % count
    valid_in = skipped[source] != devices[:, None]
    out_rank = ranked(keys[2], valid_out, entries)
    in_rank = ranked(keys[3], valid_in, entries)
    column = jnp.arange(entries, dtype=jnp.int32)[None, :]
    src_index = devices[:, None] * per_dev + out_rank
    dst_index = target * per_dev + in_rank[target, column]
    where_to = jnp.where(valid_out, src_index, BLOCKS).reshape(-1)
    table = jnp.zeros((BLOCKS + 1,), jnp.int32).at[where_to].set(dst_index.reshape(-1).astype(jnp.int32))
    return table[:BLOCKS]


def shard_levels(key, shape, cuts, smallest, high):
    loudness, own = 1.0, jax.random.fold_in(key, 6)
    for axis_at, shards_of in cuts:
        draws = jnp.exp(jax.random.uniform(jax.random.fold_in(own, axis_at), (shards_of,), jnp.float32, smallest / len(cuts), high / len(cuts)))
        loudness = loudness * jnp.repeat(draws, shape[axis_at] // shards_of).reshape([-1 if axis == axis_at else 1 for axis in range(len(shape))])
    return loudness


def profile(count, total, reach, slope):
    portions = [(1 << 20) // math.isqrt(rank ** slope) + 1 for rank in range(2, count + 1)]
    spare, counts = total - reach - (count - 1), [1] * (count - 1)
    while spare > 0:
        movable = [i for i in range(count - 1) if counts[i] < reach]
        whole, budget = sum([portions[i] for i in movable]), spare
        for i in movable:
            addition = min(reach - counts[i], max(1, budget * portions[i] // whole), spare)
            counts[i] = counts[i] + addition
            spare = spare - addition
    return np.array([reach] + counts)


def ragged(own_key, number_of, total, bound, slope):
    if number_of == 2:
        one = jax.random.randint(own_key, (), max(1, total - bound), min(bound, total - 1) + 1)
        return jnp.stack([one, total - one])
    sizes = jnp.asarray(profile(number_of, total, bound, slope), jnp.int32)
    twos = (number_of - 1) // 2
    source_of, sink = sizes[1:1 + 2 * twos:2], sizes[2:2 + 2 * twos:2]
    margin = jnp.minimum(source_of - 1, bound - sink)
    passed = jax.random.randint(jax.random.fold_in(own_key, 1), (twos,), 0, 1 << 20) % (margin + 1)
    sizes = sizes.at[1:1 + 2 * twos:2].set(source_of - passed).at[2:2 + 2 * twos:2].set(sink + passed)
    return sizes[jax.random.permutation(jax.random.fold_in(own_key, 2), number_of)]


def normal_values(rng, extent, spread, reach, shards=(), kind=jnp.bfloat16):
    loudness = shard_levels(rng, extent, shards, -0.22, 0.18) if shards else 1.0
    values = jax.random.normal(rng, extent, jnp.float32) * spread * loudness
    return jnp.minimum(jnp.maximum(values, -reach), reach).astype(kind)


def setup_inputs(seed: int = 0, part: int = 0) -> dict:
    key_of = jax.random.split(jax.random.key(seed), 10)
    own_keys = jax.random.split(jax.random.fold_in(key_of[9], part), 10)
    xbc = normal_values(own_keys[0], (TOKENS, WIDTH), 1.0, 6.0, ((0, 32),))
    dt_raw = draw_dt_raw(jax.random.fold_in(jax.random.fold_in(key_of[9], part), 71), part)
    conv_weight = normal_values(key_of[2], (KW, WIDTH), KW ** -0.5, 3.0, (), jnp.float32)
    conv_bias = normal_values(key_of[3], (WIDTH,), 0.3, 1.5, (), jnp.float32)
    dt_bias = jnp.clip(jax.random.uniform(key_of[4], (H,), jnp.float32, -4.0, -2.0), -4.0, -2.0)
    a_log = draw_a_log(jax.random.fold_in(key_of[9], 71), part)
    d_skip = jnp.clip(jax.random.uniform(key_of[6], (H,), jnp.float32, 0.5, 2.0), 0.5, 2.0)
    doc_lengths = ragged(own_keys[7], DOCS, TOKENS, TOKENS // 4, 2).astype(jnp.int32)
    loader_dest = draw_loader_dest(jax.random.fold_in(jax.random.fold_in(key_of[9], part), 71), part)
    return {"xbc": xbc, "dt_raw": dt_raw, "conv_weight": conv_weight, "conv_bias": conv_bias, "dt_bias": dt_bias, "a_log": a_log, "d_skip": d_skip, "doc_lengths": doc_lengths, "loader_dest": loader_dest}


def document_ids(doc_lengths, positions):
    ends = jnp.cumsum(doc_lengths).astype(jnp.int32)
    starts = ends - doc_lengths.astype(jnp.int32)
    return (jnp.sum((starts[None, :] <= positions[:, None]).astype(jnp.int32), axis=1) - 1).astype(jnp.int32)


def group_pieces(xpart, bpart, cpart, dtpart, ratepart, docpart, prev_doc):
    length = xpart.shape[0]
    heads = dtpart.shape[1]
    cum = jnp.cumsum(ratepart, axis=0)
    scores = jnp.dot(cpart, bpart.T, preferred_element_type=jnp.float32)
    order = jnp.arange(length, dtype=jnp.int32)
    same = (docpart[:, None] == docpart[None, :]) & (order[None, :] <= order[:, None])
    gap = jnp.minimum(cum[:, None, :] - cum[None, :, :], 0.0)
    weight = jnp.where(same[:, :, None], scores[:, :, None] * jnp.exp(gap) * dtpart[None, :, :], 0.0).astype(jnp.bfloat16)
    values = xpart.reshape(length, heads, -1).astype(jnp.float32)
    intra = jnp.einsum("tsh,shp->thp", weight.astype(jnp.float32), values, precision=lax.Precision.HIGHEST)
    last = length - 1
    tail = docpart == docpart[last]
    end_weight = jnp.where(tail[:, None], jnp.exp(cum[last][None, :] - cum) * dtpart, 0.0)
    scaled_b = (end_weight[:, :, None] * bpart.astype(jnp.float32)[:, None, :]).astype(jnp.bfloat16)
    state = jnp.einsum("shn,shp->hpn", scaled_b.astype(jnp.float32), values, precision=lax.Precision.HIGHEST)
    into = jnp.where((docpart == prev_doc)[:, None], jnp.exp(cum), 0.0)
    decay = jnp.where(docpart[last] == prev_doc, jnp.exp(cum[last]), 0.0)
    return intra, state, into, decay, values


def reference(xbc, dt_raw, conv_weight, conv_bias, dt_bias, a_log, d_skip, doc_lengths, loader_dest):
    width = xbc.shape[1]
    heads = dt_raw.shape[1]
    inner = heads * P_SIZE
    blocks = xbc.reshape(BLOCKS, BLOCK_ROWS, width)
    dt_blocks = dt_raw.reshape(BLOCKS, BLOCK_ROWS, heads)
    seq_x = jnp.zeros_like(blocks).at[loader_dest].set(blocks).reshape(TOKENS, width)
    seq_dt = jnp.zeros_like(dt_blocks).at[loader_dest].set(dt_blocks).reshape(TOKENS, heads)
    positions = jnp.arange(TOKENS, dtype=jnp.int32)
    docs = document_ids(doc_lengths, positions)
    conv = jnp.zeros((TOKENS, width), jnp.float32) + conv_bias[None, :]
    for back in range(KW):
        shifted = jnp.pad(seq_x, ((back, 0), (0, 0)))[:TOKENS]
        earlier = document_ids(doc_lengths, positions - back)
        keep = earlier == docs
        conv = conv + jnp.where(keep[:, None], conv_weight[KW - 1 - back][None, :] * shifted.astype(jnp.float32), 0.0)
    mixed = jax.nn.silu(conv).astype(jnp.bfloat16)
    xval = mixed[:, :inner]
    bmat = mixed[:, inner:inner + NS]
    cmat = mixed[:, inner + NS:]
    dt = jax.nn.softplus(seq_dt.astype(jnp.float32) + dt_bias[None, :])
    rate = -jnp.exp(a_log)[None, :] * dt
    count = TOKENS // GROUP
    prev_docs = document_ids(doc_lengths, GROUP * jnp.arange(count, dtype=jnp.int32) - 1)

    def advance(carry, pieces):
        xpart, bpart, cpart, dtpart, ratepart, docpart, prev_doc = pieces
        intra, state, into, decay, values = group_pieces(xpart, bpart, cpart, dtpart, ratepart, docpart, prev_doc)
        carried = jnp.einsum("tn,hpn->thp", cpart.astype(jnp.float32), carry, precision=lax.Precision.HIGHEST)
        total = intra + into[:, :, None] * carried + d_skip[None, :, None] * values
        return decay[:, None, None] * carry + state, total.reshape(GROUP, inner).astype(jnp.bfloat16)

    start = jnp.zeros((heads, P_SIZE, NS), jnp.float32)
    final, layer_out = lax.scan(advance, start, (xval.reshape(count, GROUP, inner), bmat.reshape(count, GROUP, NS), cmat.reshape(count, GROUP, NS), dt.reshape(count, GROUP, heads), rate.reshape(count, GROUP, heads), docs.reshape(count, GROUP), prev_docs))
    return layer_out.reshape(TOKENS, inner)
```

```python
import functools

import jax
import jax.numpy as jnp
from jax import lax
from jax.experimental import pallas as pl
from jax.experimental.pallas import tpu as pltpu
from jax.sharding import PartitionSpec as P

P_SIZE = 64
NS = 128
KW = 4
BLOCK = 128
PER_DEV = 4
LINE = 8
HALO = 16
CHUNK = 512
OFFSETS = (-2, -1, 1, 2)
SLICE = NS // LINE
MESH = pl.DeviceIdType.MESH
F32 = jnp.float32
BF16 = jnp.bfloat16


def iota(shape, axis):
    return lax.broadcasted_iota(jnp.int32, shape, axis)


def chosen(which, options):
    value = options[0]
    for number, option in enumerate(options[1:], 1):
        value = lax.select(which == number, option, value)
    return value


def split_pack(value):
    high = value.astype(BF16).astype(F32)
    return jnp.where(iota(value.shape, 1) < 64, high, value - high).astype(BF16)


def kernel(
    devices, heads,
    lens, dest, x_hbm, dt_hbm, w_ref, b_ref, par_ref,
    out_hbm,
    xin, send, recv, dtin, dtsend, dtrecv, seqx, mixed, zbuf, loc, est, sbuf, runs,
    lsend, lrecv, isend, inc, ybuf, spread, shifts, lhs, btail, fac1, fac2, rowp, rowx,
    dmine, dline, dpack,
    in_sem, dt_sem, x_send, x_recv, d_send, d_recv, h_send, h_recv, t_send, t_recv,
    s_send, s_recv, l_send, l_recv, i_send, i_recv, out_sem,
):
    inner = heads * P_SIZE
    chunks = inner // CHUNK
    me = lax.axis_index("seq")
    z = lax.rem(me, LINE)
    base = me - z

    def at(offset):
        return lax.rem(me + offset + devices, devices)

    def cols(k):
        return pl.ds(pl.multiple_of(k * CHUNK, CHUNK), CHUNK)

    tail_cols = pl.ds(inner, 2 * NS)

    def load(k):
        return pltpu.make_async_copy(x_hbm.at[:, :, cols(k)], xin.at[:, :, cols(k)], in_sem.at[k])

    load_tail = pltpu.make_async_copy(x_hbm.at[:, :, tail_cols], xin.at[:, :, tail_cols], in_sem.at[chunks])
    load_dt = pltpu.make_async_copy(dt_hbm, dtin, dt_sem.at[0])
    load_dt.start()
    load_tail.start()

    def start_load(k, carry):
        load(k).start()
        return carry

    lax.fori_loop(0, chunks, start_load, 0)

    barrier = pltpu.get_barrier_semaphore()
    partners = [at(o) for o in OFFSETS] + [base + lax.rem(z + j, LINE) for j in range(1, LINE)] + [at(LINE), at(-LINE)]
    for partner in partners:
        pl.semaphore_signal(barrier, inc=1, device_id={"seq": partner}, device_id_type=MESH)

    reach = (-2, -1, 0, 1, 2)
    own = [lax.rem(lax.shift_right_logical(dest[me * PER_DEV + j], 2) - me + 2 + devices, devices) for j in range(PER_DEV)]
    picks = []
    for number in range(5):
        pick = jnp.int32(0)
        for j in range(1, PER_DEV):
            pick = pick + jnp.where(own[j] == number, j, 0)
        picks.append(pick)
    order = {-2: 0, -1: 1, 1: 2, 2: 3, 0: 4}
    origin = [jnp.int32(0) for _ in range(PER_DEV)]
    for offset in reach:
        source = at(-offset)
        for j in range(PER_DEV):
            target = dest[source * PER_DEV + j]
            for q in range(PER_DEV):
                origin[q] = origin[q] + jnp.where(target == me * PER_DEV + q, order[offset], 0)

    def exchange(k, o, where):
        return pltpu.make_async_remote_copy(
            src_ref=send.at[o, :, where], dst_ref=recv.at[o, :, where],
            send_sem=x_send.at[o, k], recv_sem=x_recv.at[o, k],
            device_id={"seq": at(OFFSETS[o])}, device_id_type=MESH)

    def exchange_dt(o):
        return pltpu.make_async_remote_copy(
            src_ref=dtsend.at[o], dst_ref=dtrecv.at[o],
            send_sem=d_send.at[o], recv_sem=d_recv.at[o],
            device_id={"seq": at(OFFSETS[o])}, device_id_type=MESH)

    def halo(k, where):
        return pltpu.make_async_remote_copy(
            src_ref=seqx.at[pl.ds(PER_DEV * BLOCK, HALO), where], dst_ref=seqx.at[pl.ds(0, HALO), where],
            send_sem=h_send.at[k], recv_sem=h_recv.at[k],
            device_id={"seq": at(1)}, device_id_type=MESH)

    def decay_copy(j):
        return pltpu.make_async_remote_copy(
            src_ref=dmine, dst_ref=dline.at[j],
            send_sem=t_send.at[j], recv_sem=t_recv.at[j],
            device_id={"seq": base + lax.rem(z + j, LINE)}, device_id_type=MESH)

    def state_copy(k, j):
        target = lax.rem(z + j, LINE)
        return pltpu.make_async_remote_copy(
            src_ref=est.at[k, pl.ds(pl.multiple_of(target * SLICE, SLICE), SLICE)], dst_ref=sbuf.at[k, j],
            send_sem=s_send.at[k, j], recv_sem=s_recv.at[k, j],
            device_id={"seq": base + target}, device_id_type=MESH)

    def line_copy(k):
        return pltpu.make_async_remote_copy(
            src_ref=lsend.at[k], dst_ref=lrecv.at[k],
            send_sem=l_send.at[k], recv_sem=l_recv.at[k],
            device_id={"seq": at(LINE)}, device_id_type=MESH)

    def back_copy(k, j):
        target = lax.rem(z + j, LINE)
        return pltpu.make_async_remote_copy(
            src_ref=isend.at[k, j], dst_ref=inc.at[k, pl.ds(pl.multiple_of(z * SLICE, SLICE), SLICE)],
            send_sem=i_send.at[k, j], recv_sem=i_recv.at[k, j],
            device_id={"seq": base + target}, device_id_type=MESH)

    def fill(where):
        blocks = [xin[j, :, where] for j in range(PER_DEV)]
        for o, offset in enumerate(OFFSETS):
            send[o, :, where] = chosen(picks[offset + 2], blocks)
        recv[4, :, where] = chosen(picks[2], blocks)

    def place(where):
        options = [recv[o, :, where] for o in range(5)]
        for q in range(PER_DEV):
            seqx[pl.ds(HALO + q * BLOCK, BLOCK), where] = chosen(origin[q], options)

    def send_chunk(k):
        load(k).wait()
        fill(cols(k))
        for o in range(4):
            exchange(k, o, cols(k)).start()

    load_dt.wait()
    dt_blocks = [dtin[j] for j in range(PER_DEV)]
    for o, offset in enumerate(OFFSETS):
        dtsend[o] = chosen(picks[offset + 2], dt_blocks)
    dtrecv[4] = chosen(picks[2], dt_blocks)
    load_tail.wait()
    fill(tail_cols)
    pl.semaphore_wait(barrier, len(partners))
    for o in range(4):
        exchange_dt(o).start()
        exchange(chunks, o, tail_cols).start()
    send_chunk(0)
    send_chunk(1)

    starts = []
    total = jnp.int32(0)
    for n in range(lens.shape[0]):
        starts.append(total)
        total = total + lens[n]

    def docs(positions):
        found = jnp.where(starts[0] <= positions, 0, -1)
        for begin in starts[1:]:
            found = found + jnp.where(begin <= positions, 1, 0)
        return found

    row = iota((BLOCK, BLOCK), 0)
    col = iota((BLOCK, BLOCK), 1)
    square = (BLOCK, BLOCK + HALO)

    def make_shift(q, carry):
        first = (me * PER_DEV + q) * BLOCK
        same = docs(iota(square, 0) + first) == docs(iota(square, 1) + (first - HALO))
        apart = iota(square, 1) - iota(square, 0)
        for j in range(1, KW):
            keep = same & (apart == HALO - j)
            shifts[q, pl.ds((j - 1) * BLOCK, BLOCK), :] = jnp.where(keep, 1.0, 0.0).astype(BF16)
        return carry

    lax.fori_loop(0, PER_DEV, make_shift, 0)

    def make_spread(k, carry):
        head = lax.shift_right_logical(iota((128, CHUNK), 1) + k * CHUNK, 6)
        match = (iota((128, CHUNK), 0) & 63) == head
        spread[:, cols(k)] = jnp.where(match, 1.0, 0.0).astype(BF16)
        return carry

    lax.fori_loop(0, chunks, make_spread, 0)

    double = jnp.where((iota((heads, 128), 1) & 63) == iota((heads, 128), 0), 1.0, 0.0)
    params = jnp.dot(par_ref[...], double, precision=lax.Precision.HIGHEST, preferred_element_type=F32)
    lower = jnp.where(col <= row, 1.0, 0.0)

    for o in range(4):
        exchange_dt(o).wait_recv()
    through = jnp.ones((1, 128), F32)
    dt_options = [dtrecv[o] for o in range(5)]
    rows = iota((16, 128), 0)
    packed = jnp.where(rows == 12, params[2:3], 0.0)
    for q in range(PER_DEV):
        raw = jnp.dot(chosen(origin[q], dt_options), double.astype(BF16), preferred_element_type=F32) + params[0:1]
        dt = jnp.maximum(raw, 0.0) + jnp.log1p(jnp.exp(-jnp.abs(raw)))
        rate = -jnp.exp(params[1:2]) * dt
        cum = jnp.dot(lower, rate, precision=lax.Precision.HIGHEST, preferred_element_type=F32)
        last = cum[BLOCK - 1 :, :]
        middle = 0.5 * last
        fac1[q] = split_pack(jnp.exp(cum - middle))
        fac2[q] = split_pack(jnp.exp(middle - cum) * dt)
        first = (me * PER_DEV + q) * BLOCK
        on = docs(first - 1) == docs(first + BLOCK - 1)
        decay = jnp.where(jnp.broadcast_to(on, (1, 128)), jnp.exp(last), 0.0)
        packed = packed + jnp.where(rows == q, jnp.exp(middle), 0.0)
        packed = packed + jnp.where(rows == q + 4, decay, 0.0)
        packed = packed + jnp.where(rows == q + 8, through, 0.0)
        through = through * decay
    rowp[...] = split_pack(packed)
    dmine[...] = jnp.broadcast_to(through, (8, 128))
    dline[0] = dmine[...]
    for j in range(1, LINE):
        decay_copy(j).start()

    def convolved(q, where):
        window = seqx[pl.ds(pl.multiple_of(q * BLOCK, BLOCK), BLOCK + HALO), where]
        moved = jnp.dot(shifts[q], window, preferred_element_type=F32)
        weights = 0.5 * w_ref[:, where]
        half = 0.5 * b_ref[:, where] + weights[3:4] * window[HALO:].astype(F32)
        for j in range(1, KW):
            half = half + weights[3 - j : 4 - j] * moved[(j - 1) * BLOCK : j * BLOCK]
        return (half + half * jnp.tanh(half)).astype(BF16)

    for o in range(4):
        exchange(chunks, o, tail_cols).wait_recv()
    place(tail_cols)
    halo(chunks, tail_cols).start()
    halo(chunks, tail_cols).wait_recv()

    def projections(q, carry):
        both = convolved(q, tail_cols)
        bpart = both[:, :NS]
        cpart = both[:, NS:]
        first = (me * PER_DEV + q) * BLOCK
        row_docs = docs(row + first)
        scores = lax.dot_general(cpart, bpart, (((1,), (1,)), ((), ())), preferred_element_type=F32)
        keep = (row_docs == docs(col + first)) & (col <= row)
        lhs[q, :, :BLOCK] = jnp.where(keep, scores, 0.0).astype(BF16)
        enters = row_docs == docs(first - 1)
        lhs[q, :, BLOCK:] = jnp.where(enters, cpart.astype(F32), 0.0).astype(BF16)
        stays = row_docs == docs(first + BLOCK - 1)
        btail[q] = jnp.where(stays, bpart.astype(F32), 0.0).T.astype(BF16)
        return carry

    lax.fori_loop(0, PER_DEV, projections, 0)

    for j in range(1, LINE):
        decay_copy(j).wait_recv()
    line_rows = iota((8, 128), 0)
    line_decays = jnp.zeros((8, 128), F32)
    for n in range(LINE):
        line_decays = line_decays + jnp.where(line_rows == n, dline[lax.rem(z - n + LINE, LINE)], 0.0)
    dpack[...] = split_pack(jnp.concatenate([line_decays, jnp.zeros((8, 128), F32)], axis=0))

    def stage_arrive(k):
        for o in range(4):
            exchange(k, o, cols(k)).wait_recv()
        place(cols(k))
        halo(k, cols(k)).start()

    def stage_state(k):
        where = cols(k)
        halo(k, where).wait_recv()
        rowx[k] = jnp.dot(rowp[...], spread[:, where], preferred_element_type=F32)

        def block(q, state):
            loc[q, :, where] = state
            value = convolved(q, where)
            at_rows = pl.ds(pl.multiple_of(q * BLOCK, BLOCK), BLOCK)
            mixed[at_rows, where] = value
            factor = jnp.dot(fac2[q], spread[:, where], preferred_element_type=F32)
            scaled = (value.astype(F32) * factor).astype(BF16)
            zbuf[at_rows, where] = scaled
            added = jnp.dot(btail[q], scaled, preferred_element_type=F32)
            return rowx[k, pl.ds(q + 4, 1)] * state + rowx[k, pl.ds(q, 1)] * added

        state = jnp.zeros((NS, CHUNK), F32)
        for q in range(PER_DEV):
            state = block(q, state)
        est[k] = state.astype(BF16)
        for j in range(1, LINE):
            state_copy(k, j).start()
        sbuf[k, 0] = est[k, pl.ds(pl.multiple_of(z * SLICE, SLICE), SLICE)]

    def stage_prefix(k):
        for j in range(1, LINE):
            state_copy(k, j).wait_recv()
        decays = jnp.dot(dpack[...], spread[:, cols(k)], preferred_element_type=F32)
        running = jnp.zeros((SLICE, CHUNK), F32)
        for n in range(LINE):
            runs[k, n] = running
            running = decays[n : n + 1] * running + sbuf[k, lax.rem(z - n + LINE, LINE)].astype(F32)
        lsend[k] = running
        line_copy(k).start()

    def stage_back(k):
        line_copy(k).wait_recv()
        decays = jnp.dot(dpack[...], spread[:, cols(k)], preferred_element_type=F32)
        before = jnp.where(me < LINE, 0.0, lrecv[k])
        for n in range(LINE):
            isend[k, lax.rem(n - z + LINE, LINE)] = (runs[k, n] + before).astype(BF16)
            before = before * decays[n : n + 1]
        for j in range(1, LINE):
            back_copy(k, j).start()
        inc[k, pl.ds(pl.multiple_of(z * SLICE, SLICE), SLICE)] = isend[k, 0]

    def stage_out(k):
        where = cols(k)
        for j in range(1, LINE):
            back_copy(k, j).wait_recv()
        entering = inc[k].astype(F32)
        for q in range(PER_DEV):
            at_rows = pl.ds(q * BLOCK, BLOCK)
            state = loc[q, :, where] + rowx[k, pl.ds(q + 8, 1)] * entering
            scaled = (rowx[k, pl.ds(q, 1)] * state).astype(BF16)
            right = jnp.concatenate([zbuf[at_rows, where], scaled], axis=0)
            value = jnp.dot(lhs[q], right, preferred_element_type=F32)
            factor = jnp.dot(fac1[q], spread[:, where], preferred_element_type=F32)
            skip = rowx[k, pl.ds(12, 1)] * mixed[at_rows, where].astype(F32)
            ybuf[at_rows, where] = (factor * value + skip).astype(BF16)
        write(k).start()

    def write(k):
        return pltpu.make_async_copy(ybuf.at[:, cols(k)], out_hbm.at[:, cols(k)], out_sem.at[k])

    def step(i, carry):
        @pl.when(i < chunks)
        def _():
            stage_arrive(i)

        @pl.when(i + 2 < chunks)
        def _():
            send_chunk(i + 2)

        @pl.when((i >= 1) & (i - 1 < chunks))
        def _():
            stage_state(i - 1)

        @pl.when((i >= 2) & (i - 2 < chunks))
        def _():
            stage_prefix(i - 2)

        @pl.when((i >= 3) & (i - 3 < chunks))
        def _():
            stage_back(i - 3)

        @pl.when(i >= 4)
        def _():
            stage_out(i - 4)

        return carry

    lax.fori_loop(0, chunks + 4, step, 0)

    for o in range(4):
        exchange_dt(o).wait_send()
        exchange(chunks, o, tail_cols).wait_send()
    halo(chunks, tail_cols).wait_send()
    for j in range(1, LINE):
        decay_copy(j).wait_send()

    def finish(k, carry):
        for o in range(4):
            exchange(k, o, cols(k)).wait_send()
        halo(k, cols(k)).wait_send()
        line_copy(k).wait_send()
        for j in range(1, LINE):
            state_copy(k, j).wait_send()
            back_copy(k, j).wait_send()
        write(k).wait()
        return carry

    lax.fori_loop(0, chunks, finish, 0)


def body(xbc, dt_raw, conv_weight, conv_bias, dt_bias, a_log, d_skip, doc_lengths, loader_dest):
    rows, width = xbc.shape
    heads = dt_raw.shape[1]
    inner = heads * P_SIZE
    chunks = inner // CHUNK
    devices = lax.axis_size("seq")
    params = jnp.concatenate(
        [dt_bias[None], a_log[None], d_skip[None], jnp.zeros((5, heads), F32)], axis=0)
    vmem = pl.BlockSpec(memory_space=pltpu.VMEM)
    smem = pl.BlockSpec(memory_space=pltpu.SMEM)
    anywhere = pl.BlockSpec(memory_space=pl.ANY)
    dma = pltpu.SemaphoreType.DMA
    V = pltpu.VMEM
    scratch = [
        V((PER_DEV, BLOCK, width), BF16),
        V((4, BLOCK, width), BF16),
        V((5, BLOCK, width), BF16),
        V((PER_DEV, BLOCK, heads), BF16),
        V((4, BLOCK, heads), BF16),
        V((5, BLOCK, heads), BF16),
        V((HALO + rows, width), BF16),
        V((rows, inner), BF16),
        V((rows, inner), BF16),
        V((PER_DEV, NS, inner), F32),
        V((chunks, NS, CHUNK), BF16),
        V((chunks, LINE, SLICE, CHUNK), BF16),
        V((chunks, LINE, SLICE, CHUNK), F32),
        V((chunks, SLICE, CHUNK), F32),
        V((chunks, SLICE, CHUNK), F32),
        V((chunks, LINE, SLICE, CHUNK), BF16),
        V((chunks, NS, CHUNK), BF16),
        V((rows, inner), BF16),
        V((128, inner), BF16),
        V((PER_DEV, (KW - 1) * BLOCK, BLOCK + HALO), BF16),
        V((PER_DEV, BLOCK, BLOCK + NS), BF16),
        V((PER_DEV, NS, BLOCK), BF16),
        V((PER_DEV, BLOCK, 128), BF16),
        V((PER_DEV, BLOCK, 128), BF16),
        V((16, 128), BF16),
        V((chunks, 16, CHUNK), F32),
        V((8, 128), F32),
        V((LINE, 8, 128), F32),
        V((16, 128), BF16),
        dma((chunks + 1,)), dma((1,)),
        dma((4, chunks + 1)), dma((4, chunks + 1)),
        dma((4,)), dma((4,)),
        dma((chunks + 1,)), dma((chunks + 1,)),
        dma((LINE,)), dma((LINE,)),
        dma((chunks, LINE)), dma((chunks, LINE)),
        dma((chunks,)), dma((chunks,)),
        dma((chunks, LINE)), dma((chunks, LINE)),
        dma((chunks,)),
    ]
    return pl.pallas_call(
        functools.partial(kernel, devices, heads),
        out_shape=jax.ShapeDtypeStruct((rows, inner), BF16),
        in_specs=[smem, smem, anywhere, anywhere, vmem, vmem, vmem],
        out_specs=anywhere,
        scratch_shapes=scratch,
        cost_estimate=pl.CostEstimate(flops=2_000_000_000, bytes_accessed=10_000_000, transcendentals=3_000_000),
        compiler_params=pltpu.CompilerParams(
            collective_id=0, has_side_effects=True, vmem_limit_bytes=56 * 1024 * 1024),
    )(
        doc_lengths, loader_dest,
        xbc.reshape(PER_DEV, BLOCK, width), dt_raw.reshape(PER_DEV, BLOCK, heads),
        conv_weight, conv_bias.reshape(1, width), params,
    )


def solution(mesh):
    placed = (
        P(("dp", "seq"), None),
        P(("dp", "seq"), None),
        P(),
        P(),
        P(),
        P(),
        P(),
        P("dp"),
        P("dp"),
    )
    return jax.shard_map(
        body, mesh=mesh, in_specs=placed, out_specs=P(("dp", "seq"), None), check_vma=False
    )
```

```python
import functools

import jax
import jax.numpy as jnp
from jax import lax
from jax.experimental import pallas as pl
from jax.experimental.pallas import tpu as pltpu
from jax.sharding import PartitionSpec as P

P_SIZE = 64
NS = 128
KW = 4
BLOCK = 128
PER_DEV = 4
LINE = 8
HALO = 16
CHUNK = 512
AHEAD = 2
LAGS = (1, 3, 6, 9)
OFFSETS = (-2, -1, 1, 2)
SLICE = NS // LINE
MESH = pl.DeviceIdType.MESH
F32 = jnp.float32
BF16 = jnp.bfloat16


def iota(shape, axis):
    return lax.broadcasted_iota(jnp.int32, shape, axis)


def chosen(which, options):
    value = options[0]
    for number, option in enumerate(options[1:], 1):
        value = lax.select(which == number, option, value)
    return value


def split_pack(value):
    high = value.astype(BF16).astype(F32)
    return jnp.where(iota(value.shape, 1) < 64, high, value - high).astype(BF16)


def kernel(
    devices, heads,
    lens, dest, x_hbm, dt_hbm, w_ref, b_ref, dtb_ref, alog_ref, skip_ref,
    out_hbm,
    xin, send, recv, dtin, dtsend, dtrecv, seqx, mixed, zbuf, loc, est, sbuf, runs,
    lsend, lrecv, isend, inc, ybuf, spread, shifts, lhs, btail, fac1, fac2, rowp, rowx,
    dmine, dline, dpack,
    in_sem, dt_sem, x_send, x_recv, d_send, d_recv, h_send, h_recv, t_send, t_recv,
    s_send, s_recv, l_send, l_recv, i_send, i_recv, out_sem,
):
    inner = heads * P_SIZE
    chunks = inner // CHUNK
    me = lax.axis_index("seq")
    z = lax.rem(me, LINE)
    base = me - z

    def at(offset):
        return lax.rem(me + offset + devices, devices)

    def cols(k):
        return pl.ds(pl.multiple_of(k * CHUNK, CHUNK), CHUNK)

    tail_cols = pl.ds(inner, 2 * NS)

    def load(k):
        return pltpu.make_async_copy(x_hbm.at[:, :, cols(k)], xin.at[:, :, cols(k)], in_sem.at[k])

    load_tail = pltpu.make_async_copy(x_hbm.at[:, :, tail_cols], xin.at[:, :, tail_cols], in_sem.at[chunks])
    load_dt = pltpu.make_async_copy(dt_hbm, dtin, dt_sem.at[0])
    load_dt.start()
    load_tail.start()

    def start_load(k, carry):
        load(k).start()
        return carry

    lax.fori_loop(0, chunks, start_load, 0)

    barrier = pltpu.get_barrier_semaphore()
    partners = [at(o) for o in OFFSETS] + [base + lax.rem(z + j, LINE) for j in range(1, LINE)] + [at(LINE), at(-LINE)]
    for partner in partners:
        pl.semaphore_signal(barrier, inc=1, device_id={"seq": partner}, device_id_type=MESH)

    reach = (-2, -1, 0, 1, 2)
    own = [lax.rem(lax.shift_right_logical(dest[me * PER_DEV + j], 2) - me + 2 + devices, devices) for j in range(PER_DEV)]
    picks = []
    for number in range(5):
        pick = jnp.int32(0)
        for j in range(1, PER_DEV):
            pick = pick + jnp.where(own[j] == number, j, 0)
        picks.append(pick)
    order = {-2: 0, -1: 1, 1: 2, 2: 3, 0: 4}
    origin = [jnp.int32(0) for _ in range(PER_DEV)]
    for offset in reach:
        source = at(-offset)
        for j in range(PER_DEV):
            target = dest[source * PER_DEV + j]
            for q in range(PER_DEV):
                origin[q] = origin[q] + jnp.where(target == me * PER_DEV + q, order[offset], 0)

    def exchange(k, o, where):
        return pltpu.make_async_remote_copy(
            src_ref=send.at[o, :, where], dst_ref=recv.at[o, :, where],
            send_sem=x_send.at[o, k], recv_sem=x_recv.at[o, k],
            device_id={"seq": at(OFFSETS[o])}, device_id_type=MESH)

    def exchange_dt(o):
        return pltpu.make_async_remote_copy(
            src_ref=dtsend.at[o], dst_ref=dtrecv.at[o],
            send_sem=d_send.at[o], recv_sem=d_recv.at[o],
            device_id={"seq": at(OFFSETS[o])}, device_id_type=MESH)

    def halo(k, where):
        return pltpu.make_async_remote_copy(
            src_ref=seqx.at[pl.ds(PER_DEV * BLOCK, HALO), where], dst_ref=seqx.at[pl.ds(0, HALO), where],
            send_sem=h_send.at[k], recv_sem=h_recv.at[k],
            device_id={"seq": at(1)}, device_id_type=MESH)

    def decay_copy(j):
        return pltpu.make_async_remote_copy(
            src_ref=dmine, dst_ref=dline.at[j],
            send_sem=t_send.at[j], recv_sem=t_recv.at[j],
            device_id={"seq": base + lax.rem(z + j, LINE)}, device_id_type=MESH)

    def state_copy(k, j):
        target = lax.rem(z + j, LINE)
        return pltpu.make_async_remote_copy(
            src_ref=est.at[k, pl.ds(pl.multiple_of(target * SLICE, SLICE), SLICE)], dst_ref=sbuf.at[k, j],
            send_sem=s_send.at[k, j], recv_sem=s_recv.at[k, j],
            device_id={"seq": base + target}, device_id_type=MESH)

    def line_copy(k):
        return pltpu.make_async_remote_copy(
            src_ref=lsend.at[k], dst_ref=lrecv.at[k],
            send_sem=l_send.at[k], recv_sem=l_recv.at[k],
            device_id={"seq": at(LINE)}, device_id_type=MESH)

    def back_copy(k, j):
        target = lax.rem(z + j, LINE)
        return pltpu.make_async_remote_copy(
            src_ref=isend.at[k, j], dst_ref=inc.at[k, pl.ds(pl.multiple_of(z * SLICE, SLICE), SLICE)],
            send_sem=i_send.at[k, j], recv_sem=i_recv.at[k, j],
            device_id={"seq": base + target}, device_id_type=MESH)

    def fill(where):
        blocks = [xin[j, :, where] for j in range(PER_DEV)]
        for o, offset in enumerate(OFFSETS):
            send[o, :, where] = chosen(picks[offset + 2], blocks)
        recv[4, :, where] = chosen(picks[2], blocks)

    def place(where):
        options = [recv[o, :, where] for o in range(5)]
        for q in range(PER_DEV):
            seqx[pl.ds(HALO + q * BLOCK, BLOCK), where] = chosen(origin[q], options)

    def send_chunk(k):
        load(k).wait()
        fill(cols(k))
        for o in range(4):
            exchange(k, o, cols(k)).start()

    load_dt.wait()
    dt_blocks = [dtin[:, j * BLOCK : (j + 1) * BLOCK] for j in range(PER_DEV)]
    for o, offset in enumerate(OFFSETS):
        dtsend[o] = chosen(picks[offset + 2], dt_blocks)
    dtrecv[4] = chosen(picks[2], dt_blocks)
    load_tail.wait()
    fill(tail_cols)
    pl.semaphore_wait(barrier, len(partners))
    for o in range(4):
        exchange_dt(o).start()
        exchange(chunks, o, tail_cols).start()
    for k in range(AHEAD):
        send_chunk(k)

    starts = []
    total = jnp.int32(0)
    for n in range(lens.shape[0]):
        starts.append(total)
        total = total + lens[n]

    def docs(positions):
        found = jnp.where(starts[0] <= positions, 0, -1)
        for begin in starts[1:]:
            found = found + jnp.where(begin <= positions, 1, 0)
        return found

    row = iota((BLOCK, BLOCK), 0)
    col = iota((BLOCK, BLOCK), 1)
    square = (BLOCK, BLOCK + HALO)

    def make_shift(q, carry):
        first = (me * PER_DEV + q) * BLOCK
        same = docs(iota((BLOCK, 1), 0) + first) == docs(iota((1, BLOCK + HALO), 1) + (first - HALO))
        apart = iota(square, 1) - iota(square, 0)
        for j in range(1, KW):
            keep = same & (apart == HALO - j)
            shifts[q, pl.ds((j - 1) * BLOCK, BLOCK), :] = jnp.where(keep, 1.0, 0.0).astype(BF16)
        return carry

    lax.fori_loop(0, PER_DEV, make_shift, 0)

    def make_spread(k, carry):
        head = lax.shift_right_logical(iota((128, CHUNK), 1) + k * CHUNK, 6)
        match = (iota((128, CHUNK), 0) & 63) == head
        spread[:, cols(k)] = jnp.where(match, 1.0, 0.0).astype(BF16)
        return carry

    lax.fori_loop(0, chunks, make_spread, 0)

    double = jnp.where((iota((heads, 128), 1) & 63) == iota((heads, 128), 0), 1.0, 0.0)
    which = iota((8, heads), 0)
    stacked = jnp.where(which == 0, dtb_ref[...], jnp.where(which == 1, alog_ref[...], skip_ref[...]))
    params = jnp.dot(stacked, double, precision=lax.Precision.HIGHEST, preferred_element_type=F32)
    lower = jnp.where(col <= row, 1.0, 0.0)

    for o in range(4):
        exchange_dt(o).wait_recv()
    through = jnp.ones((1, 128), F32)
    dt_options = [dtrecv[o] for o in range(5)]
    rows = iota((16, 128), 0)
    packed = jnp.where(rows == 12, params[2:3], 0.0)
    for q in range(PER_DEV):
        raw = lax.dot_general(
            chosen(origin[q], dt_options), double.astype(BF16), (((0,), (0,)), ((), ())),
            preferred_element_type=F32) + params[0:1]
        dt = jnp.maximum(raw, 0.0) + jnp.log1p(jnp.exp(-jnp.abs(raw)))
        rate = -jnp.exp(params[1:2]) * dt
        cum = jnp.dot(lower, rate, precision=lax.Precision.HIGHEST, preferred_element_type=F32)
        last = cum[BLOCK - 1 :, :]
        middle = 0.5 * last
        fac1[q] = split_pack(jnp.exp(cum - middle))
        fac2[q] = split_pack(jnp.exp(middle - cum) * dt)
        first = (me * PER_DEV + q) * BLOCK
        on = docs(first - 1) == docs(first + BLOCK - 1)
        decay = jnp.where(jnp.broadcast_to(on, (1, 128)), jnp.exp(last), 0.0)
        packed = packed + jnp.where(rows == q, jnp.exp(middle), 0.0)
        packed = packed + jnp.where(rows == q + 4, decay, 0.0)
        packed = packed + jnp.where(rows == q + 8, through, 0.0)
        through = through * decay
    rowp[...] = split_pack(packed)
    dmine[...] = jnp.broadcast_to(through, (8, 128))
    dline[0] = dmine[...]
    for j in range(1, LINE):
        decay_copy(j).start()

    def convolved(q, where):
        window = seqx[pl.ds(pl.multiple_of(q * BLOCK, BLOCK), BLOCK + HALO), where]
        moved = jnp.dot(shifts[q], window, preferred_element_type=F32)
        weights = 0.5 * w_ref[:, where]
        half = 0.5 * b_ref[where].reshape(1, -1) + weights[3:4] * window[HALO:].astype(F32)
        for j in range(1, KW):
            half = half + weights[3 - j : 4 - j] * moved[(j - 1) * BLOCK : j * BLOCK]
        return (half + half * jnp.tanh(half)).astype(BF16)

    for o in range(4):
        exchange(chunks, o, tail_cols).wait_recv()
    place(tail_cols)
    halo(chunks, tail_cols).start()

    def projections(q, carry):
        both = convolved(q, tail_cols)
        bpart = both[:, :NS]
        cpart = both[:, NS:]
        first = (me * PER_DEV + q) * BLOCK
        row_docs = docs(iota((BLOCK, 1), 0) + first)
        scores = lax.dot_general(cpart, bpart, (((1,), (1,)), ((), ())), preferred_element_type=F32)
        keep = (row_docs == docs(iota((1, BLOCK), 1) + first)) & (col <= row)
        lhs[q, :, :BLOCK] = jnp.where(keep, scores, 0.0).astype(BF16)
        enters = row_docs == docs(first - 1)
        lhs[q, :, BLOCK:] = jnp.where(enters, cpart.astype(F32), 0.0).astype(BF16)
        stays = row_docs == docs(first + BLOCK - 1)
        btail[q] = jnp.where(stays, bpart.astype(F32), 0.0).T.astype(BF16)
        return carry

    def prepare_projections():
        halo(chunks, tail_cols).wait_recv()
        lax.fori_loop(0, PER_DEV, projections, 0)

    def prepare_decays():
        for j in range(1, LINE):
            decay_copy(j).wait_recv()
        line_rows = iota((8, 128), 0)
        line_decays = jnp.zeros((8, 128), F32)
        for n in range(LINE):
            line_decays = line_decays + jnp.where(line_rows == n, dline[lax.rem(z - n + LINE, LINE)], 0.0)
        dpack[...] = split_pack(jnp.concatenate([line_decays, jnp.zeros((8, 128), F32)], axis=0))

    def stage_arrive(k):
        for o in range(4):
            exchange(k, o, cols(k)).wait_recv()
        place(cols(k))
        halo(k, cols(k)).start()

    def stage_state(k):
        where = cols(k)
        halo(k, where).wait_recv()
        rowx[k] = jnp.dot(rowp[...], spread[:, where], preferred_element_type=F32)

        def block(q, state):
            loc[q, :, where] = state
            value = convolved(q, where)
            at_rows = pl.ds(pl.multiple_of(q * BLOCK, BLOCK), BLOCK)
            mixed[at_rows, where] = value
            factor = jnp.dot(fac2[q], spread[:, where], preferred_element_type=F32)
            scaled = (value.astype(F32) * factor).astype(BF16)
            zbuf[at_rows, where] = scaled
            added = jnp.dot(btail[q], scaled, preferred_element_type=F32)
            return rowx[k, pl.ds(q + 4, 1)] * state + rowx[k, pl.ds(q, 1)] * added

        state = jnp.zeros((NS, CHUNK), F32)
        for q in range(PER_DEV):
            state = block(q, state)
        est[k] = state.astype(BF16)
        for j in range(1, LINE):
            state_copy(k, j).start()
        sbuf[k, 0] = est[k, pl.ds(pl.multiple_of(z * SLICE, SLICE), SLICE)]

    def stage_prefix(k):
        for j in range(1, LINE):
            state_copy(k, j).wait_recv()
        decays = jnp.dot(dpack[...], spread[:, cols(k)], preferred_element_type=F32)
        running = jnp.zeros((SLICE, CHUNK), F32)
        for n in range(LINE):
            runs[k, n] = running
            running = decays[n : n + 1] * running + sbuf[k, lax.rem(z - n + LINE, LINE)].astype(F32)
        lsend[k] = running
        line_copy(k).start()

    def stage_back(k):
        line_copy(k).wait_recv()
        decays = jnp.dot(dpack[...], spread[:, cols(k)], preferred_element_type=F32)
        before = jnp.where(me < LINE, 0.0, lrecv[k])
        for n in range(LINE):
            isend[k, lax.rem(n - z + LINE, LINE)] = (runs[k, n] + before).astype(BF16)
            before = before * decays[n : n + 1]
        for j in range(1, LINE):
            back_copy(k, j).start()
        inc[k, pl.ds(pl.multiple_of(z * SLICE, SLICE), SLICE)] = isend[k, 0]

    def stage_out(k):
        where = cols(k)
        for j in range(1, LINE):
            back_copy(k, j).wait_recv()
        entering = inc[k].astype(F32)
        for q in range(PER_DEV):
            at_rows = pl.ds(q * BLOCK, BLOCK)
            state = loc[q, :, where] + rowx[k, pl.ds(q + 8, 1)] * entering
            scaled = (rowx[k, pl.ds(q, 1)] * state).astype(BF16)
            right = jnp.concatenate([zbuf[at_rows, where], scaled], axis=0)
            value = jnp.dot(lhs[q], right, preferred_element_type=F32)
            factor = jnp.dot(fac1[q], spread[:, where], preferred_element_type=F32)
            skip = rowx[k, pl.ds(12, 1)] * mixed[at_rows, where].astype(F32)
            ybuf[at_rows, where] = (factor * value + skip).astype(BF16)
        write(k).start()

    def write(k):
        return pltpu.make_async_copy(ybuf.at[:, cols(k)], out_hbm.at[:, cols(k)], out_sem.at[k])

    def step(i, carry):
        @pl.when(i < chunks)
        def _():
            stage_arrive(i)

        pl.when(i == LAGS[0])(prepare_projections)

        @pl.when((i >= LAGS[0]) & (i - LAGS[0] < chunks))
        def _():
            stage_state(i - LAGS[0])

        pl.when(i == LAGS[1])(prepare_decays)

        @pl.when((i >= LAGS[1]) & (i - LAGS[1] < chunks))
        def _():
            stage_prefix(i - LAGS[1])

        @pl.when((i >= LAGS[2]) & (i - LAGS[2] < chunks))
        def _():
            stage_back(i - LAGS[2])

        @pl.when(i + AHEAD < chunks)
        def _():
            send_chunk(i + AHEAD)

        @pl.when((i >= LAGS[3]) & (i - LAGS[3] < chunks))
        def _():
            stage_out(i - LAGS[3])

        return carry

    lax.fori_loop(0, chunks + LAGS[-1], step, 0)

    for o in range(4):
        exchange_dt(o).wait_send()
        exchange(chunks, o, tail_cols).wait_send()
    halo(chunks, tail_cols).wait_send()
    for j in range(1, LINE):
        decay_copy(j).wait_send()

    def finish(k, carry):
        for o in range(4):
            exchange(k, o, cols(k)).wait_send()
        halo(k, cols(k)).wait_send()
        line_copy(k).wait_send()
        for j in range(1, LINE):
            state_copy(k, j).wait_send()
            back_copy(k, j).wait_send()
        write(k).wait()
        return carry

    lax.fori_loop(0, chunks, finish, 0)


def body(xbc, dt_raw, conv_weight, conv_bias, dt_bias, a_log, d_skip, doc_lengths, loader_dest):
    rows, width = xbc.shape
    heads = dt_raw.shape[1]
    inner = heads * P_SIZE
    chunks = inner // CHUNK
    devices = lax.axis_size("seq")
    vmem = pl.BlockSpec(memory_space=pltpu.VMEM)
    smem = pl.BlockSpec(memory_space=pltpu.SMEM)
    anywhere = pl.BlockSpec(memory_space=pl.ANY)
    dma = pltpu.SemaphoreType.DMA
    V = pltpu.VMEM
    scratch = [
        V((PER_DEV, BLOCK, width), BF16),
        V((4, BLOCK, width), BF16),
        V((5, BLOCK, width), BF16),
        V((heads, rows), BF16),
        V((4, heads, BLOCK), BF16),
        V((5, heads, BLOCK), BF16),
        V((HALO + rows, width), BF16),
        V((rows, inner), BF16),
        V((rows, inner), BF16),
        V((PER_DEV, NS, inner), F32),
        V((chunks, NS, CHUNK), BF16),
        V((chunks, LINE, SLICE, CHUNK), BF16),
        V((chunks, LINE, SLICE, CHUNK), F32),
        V((chunks, SLICE, CHUNK), F32),
        V((chunks, SLICE, CHUNK), F32),
        V((chunks, LINE, SLICE, CHUNK), BF16),
        V((chunks, NS, CHUNK), BF16),
        V((rows, inner), BF16),
        V((128, inner), BF16),
        V((PER_DEV, (KW - 1) * BLOCK, BLOCK + HALO), BF16),
        V((PER_DEV, BLOCK, BLOCK + NS), BF16),
        V((PER_DEV, NS, BLOCK), BF16),
        V((PER_DEV, BLOCK, 128), BF16),
        V((PER_DEV, BLOCK, 128), BF16),
        V((16, 128), BF16),
        V((chunks, 16, CHUNK), F32),
        V((8, 128), F32),
        V((LINE, 8, 128), F32),
        V((16, 128), BF16),
        dma((chunks + 1,)), dma((1,)),
        dma((4, chunks + 1)), dma((4, chunks + 1)),
        dma((4,)), dma((4,)),
        dma((chunks + 1,)), dma((chunks + 1,)),
        dma((LINE,)), dma((LINE,)),
        dma((chunks, LINE)), dma((chunks, LINE)),
        dma((chunks,)), dma((chunks,)),
        dma((chunks, LINE)), dma((chunks, LINE)),
        dma((chunks,)),
    ]
    return pl.pallas_call(
        functools.partial(kernel, devices, heads),
        out_shape=jax.ShapeDtypeStruct((rows, inner), BF16),
        in_specs=[smem, smem, anywhere, anywhere, vmem, vmem, vmem, vmem, vmem],
        out_specs=anywhere,
        scratch_shapes=scratch,
        cost_estimate=pl.CostEstimate(flops=2_000_000_000, bytes_accessed=10_000_000, transcendentals=3_000_000),
        compiler_params=pltpu.CompilerParams(
            collective_id=0, has_side_effects=True, vmem_limit_bytes=63 * 1024 * 1024),
    )(
        doc_lengths, loader_dest,
        xbc.reshape(PER_DEV, BLOCK, width), dt_raw.T,
        conv_weight, conv_bias, dt_bias[None], a_log[None], d_skip[None],
    )


def solution(mesh):
    placed = (
        P(("dp", "seq"), None),
        P(("dp", "seq"), None),
        P(),
        P(),
        P(),
        P(),
        P(),
        P("dp"),
        P("dp"),
    )
    return jax.shard_map(
        body, mesh=mesh, in_specs=placed, out_specs=P(("dp", "seq"), None), check_vma=False
    )
```

```python
import functools

import jax
import jax.numpy as jnp
from jax import lax
from jax.experimental import pallas as pl
from jax.experimental.pallas import tpu as pltpu
from jax.sharding import PartitionSpec as P

P_SIZE = 64
NS = 128
KW = 4
BLOCK = 128
PER_DEV = 4
LINE = 8
HALO = 16
CHUNK = 512
AHEAD = 2
LAGS = (1, 2, 4, 6, 8, 10)
OFFSETS = (-2, -1, 1, 2)
SLICE = NS // LINE
PAIRS = LINE // 2
MESH = pl.DeviceIdType.MESH
F32 = jnp.float32
BF16 = jnp.bfloat16


def iota(shape, axis):
    return lax.broadcasted_iota(jnp.int32, shape, axis)


def chosen(which, options):
    value = options[0]
    for number, option in enumerate(options[1:], 1):
        value = lax.select(which == number, option, value)
    return value


def split_pack(value):
    high = value.astype(BF16).astype(F32)
    return jnp.where(iota(value.shape, 1) < 64, high, value - high).astype(BF16)


def kernel(
    devices, heads,
    lens, dest, x_hbm, dt_hbm, w_ref, b_ref, dtb_ref, alog_ref, skip_ref,
    out_hbm,
    xin, send, recv, dtin, dtsend, dtrecv, seqx, mixed, zbuf, loc, est, est32, sin, sbuf, runs,
    lsend, lrecv, isend, rsend, inc, ybuf, spread, shifts, lhs, btail, fac1, fac2, rowp, rowx,
    dmine, dline, dpack, decx,
    in_sem, dt_sem, x_send, x_recv, d_send, d_recv, h_send, h_recv, t_send, t_recv,
    s_send, s_recv, l_send, l_recv, i_send, i_recv, p_send, p_recv, r_send, r_recv, out_sem,
):
    inner = heads * P_SIZE
    chunks = inner // CHUNK
    me = lax.axis_index("seq")
    z = lax.rem(me - lax.rem(lax.axis_index("dp"), 2) + devices, LINE)
    pair = lax.shift_right_logical(z, 1)
    even = lax.rem(z, 2) == 0
    odd = lax.rem(z, 2) == 1

    def at(offset):
        return lax.rem(me + offset + devices, devices)

    def member(place):
        return at(place - z)

    def cols(k):
        return pl.ds(pl.multiple_of(k * CHUNK, CHUNK), CHUNK)

    tail_cols = pl.ds(inner, 2 * NS)

    def load(k):
        return pltpu.make_async_copy(x_hbm.at[:, :, cols(k)], xin.at[:, :, cols(k)], in_sem.at[k])

    load_tail = pltpu.make_async_copy(x_hbm.at[:, :, tail_cols], xin.at[:, :, tail_cols], in_sem.at[chunks])
    load_dt = pltpu.make_async_copy(dt_hbm, dtin, dt_sem.at[0])
    load_dt.start()
    load_tail.start()

    def start_load(k, carry):
        load(k).start()
        return carry

    lax.fori_loop(0, chunks, start_load, 0)

    barrier = pltpu.get_barrier_semaphore()
    partners = [at(o) for o in OFFSETS] + [member(lax.rem(z + j, LINE)) for j in range(1, LINE)] + [at(LINE), at(-LINE)]
    for partner in partners:
        pl.semaphore_signal(barrier, inc=1, device_id={"seq": partner}, device_id_type=MESH)

    reach = (-2, -1, 0, 1, 2)
    own = [lax.rem(lax.shift_right_logical(dest[me * PER_DEV + j], 2) - me + 2 + devices, devices) for j in range(PER_DEV)]
    picks = []
    for number in range(5):
        pick = jnp.int32(0)
        for j in range(1, PER_DEV):
            pick = pick + jnp.where(own[j] == number, j, 0)
        picks.append(pick)
    order = {-2: 0, -1: 1, 1: 2, 2: 3, 0: 4}
    origin = [jnp.int32(0) for _ in range(PER_DEV)]
    for offset in reach:
        source = at(-offset)
        for j in range(PER_DEV):
            target = dest[source * PER_DEV + j]
            for q in range(PER_DEV):
                origin[q] = origin[q] + jnp.where(target == me * PER_DEV + q, order[offset], 0)

    def exchange(k, o, where):
        return pltpu.make_async_remote_copy(
            src_ref=send.at[o, :, where], dst_ref=recv.at[o, :, where],
            send_sem=x_send.at[o, k], recv_sem=x_recv.at[o, k],
            device_id={"seq": at(OFFSETS[o])}, device_id_type=MESH)

    def exchange_dt(o):
        return pltpu.make_async_remote_copy(
            src_ref=dtsend.at[o], dst_ref=dtrecv.at[o],
            send_sem=d_send.at[o], recv_sem=d_recv.at[o],
            device_id={"seq": at(OFFSETS[o])}, device_id_type=MESH)

    def halo(k, where):
        return pltpu.make_async_remote_copy(
            src_ref=seqx.at[pl.ds(PER_DEV * BLOCK, HALO), where], dst_ref=seqx.at[pl.ds(0, HALO), where],
            send_sem=h_send.at[k], recv_sem=h_recv.at[k],
            device_id={"seq": at(1)}, device_id_type=MESH)

    def decay_copy(j):
        return pltpu.make_async_remote_copy(
            src_ref=dmine, dst_ref=dline.at[j],
            send_sem=t_send.at[j], recv_sem=t_recv.at[j],
            device_id={"seq": member(lax.rem(z + j, LINE))}, device_id_type=MESH)

    def pair_copy(k):
        return pltpu.make_async_remote_copy(
            src_ref=est.at[k], dst_ref=sin.at[k],
            send_sem=p_send.at[k], recv_sem=p_recv.at[k],
            device_id={"seq": at(-1)}, device_id_type=MESH)

    def relay_copy(k):
        return pltpu.make_async_remote_copy(
            src_ref=rsend.at[k], dst_ref=inc.at[k],
            send_sem=r_send.at[k], recv_sem=r_recv.at[k],
            device_id={"seq": at(1)}, device_id_type=MESH)

    def state_copy(k, j, sender):
        target = lax.rem(z + j, LINE)
        return pltpu.make_async_remote_copy(
            src_ref=est.at[k, pl.ds(pl.multiple_of(target * SLICE, SLICE), SLICE)], dst_ref=sbuf.at[k, sender],
            send_sem=s_send.at[k, j], recv_sem=s_recv.at[k, sender],
            device_id={"seq": member(target)}, device_id_type=MESH)

    def line_copy(k):
        return pltpu.make_async_remote_copy(
            src_ref=lsend.at[k], dst_ref=lrecv.at[k],
            send_sem=l_send.at[k], recv_sem=l_recv.at[k],
            device_id={"seq": at(LINE)}, device_id_type=MESH)

    def back_copy(k, p, sender):
        return pltpu.make_async_remote_copy(
            src_ref=isend.at[k, p], dst_ref=inc.at[k, pl.ds(pl.multiple_of(sender * SLICE, SLICE), SLICE)],
            send_sem=i_send.at[k, p], recv_sem=i_recv.at[k, sender],
            device_id={"seq": member(2 * p)}, device_id_type=MESH)

    def fill(where):
        blocks = [xin[j, :, where] for j in range(PER_DEV)]
        for o, offset in enumerate(OFFSETS):
            send[o, :, where] = chosen(picks[offset + 2], blocks)
        recv[4, :, where] = chosen(picks[2], blocks)

    def place(where):
        options = [recv[o, :, where] for o in range(5)]
        for q in range(PER_DEV):
            seqx[pl.ds(HALO + q * BLOCK, BLOCK), where] = chosen(origin[q], options)

    def send_chunk(k):
        load(k).wait()
        fill(cols(k))
        for o in range(4):
            exchange(k, o, cols(k)).start()

    load_dt.wait()
    dt_blocks = [dtin[:, j * BLOCK : (j + 1) * BLOCK] for j in range(PER_DEV)]
    for o, offset in enumerate(OFFSETS):
        dtsend[o] = chosen(picks[offset + 2], dt_blocks)
    dtrecv[4] = chosen(picks[2], dt_blocks)
    load_tail.wait()
    fill(tail_cols)
    pl.semaphore_wait(barrier, len(partners))
    for o in range(4):
        exchange_dt(o).start()
        exchange(chunks, o, tail_cols).start()
    for k in range(AHEAD):
        send_chunk(k)

    starts = []
    total = jnp.int32(0)
    for n in range(lens.shape[0]):
        starts.append(total)
        total = total + lens[n]

    def docs(positions):
        found = jnp.where(starts[0] <= positions, 0, -1)
        for begin in starts[1:]:
            found = found + jnp.where(begin <= positions, 1, 0)
        return found

    row = iota((BLOCK, BLOCK), 0)
    col = iota((BLOCK, BLOCK), 1)
    square = (BLOCK, BLOCK + HALO)

    def make_shift(q, carry):
        first = (me * PER_DEV + q) * BLOCK
        same = docs(iota((BLOCK, 1), 0) + first) == docs(iota((1, BLOCK + HALO), 1) + (first - HALO))
        apart = iota(square, 1) - iota(square, 0)
        for j in range(1, KW):
            keep = same & (apart == HALO - j)
            shifts[q, pl.ds((j - 1) * BLOCK, BLOCK), :] = jnp.where(keep, 1.0, 0.0).astype(BF16)
        return carry

    lax.fori_loop(0, PER_DEV, make_shift, 0)

    def make_spread(k, carry):
        head = lax.shift_right_logical(iota((128, CHUNK), 1) + k * CHUNK, 6)
        match = (iota((128, CHUNK), 0) & 63) == head
        spread[:, cols(k)] = jnp.where(match, 1.0, 0.0).astype(BF16)
        return carry

    lax.fori_loop(0, chunks, make_spread, 0)

    double = jnp.where((iota((heads, 128), 1) & 63) == iota((heads, 128), 0), 1.0, 0.0)
    which = iota((8, heads), 0)
    stacked = jnp.where(which == 0, dtb_ref[...], jnp.where(which == 1, alog_ref[...], skip_ref[...]))
    params = jnp.dot(stacked, double, precision=lax.Precision.HIGHEST, preferred_element_type=F32)
    lower = jnp.where(col <= row, 1.0, 0.0)

    for o in range(4):
        exchange_dt(o).wait_recv()
    through = jnp.ones((1, 128), F32)
    dt_options = [dtrecv[o] for o in range(5)]
    rows = iota((16, 128), 0)
    packed = jnp.where(rows == 12, params[2:3], 0.0)
    for q in range(PER_DEV):
        raw = lax.dot_general(
            chosen(origin[q], dt_options), double.astype(BF16), (((0,), (0,)), ((), ())),
            preferred_element_type=F32) + params[0:1]
        dt = jnp.maximum(raw, 0.0) + jnp.log1p(jnp.exp(-jnp.abs(raw)))
        rate = -jnp.exp(params[1:2]) * dt
        cum = jnp.dot(lower, rate, precision=lax.Precision.HIGHEST, preferred_element_type=F32)
        last = cum[BLOCK - 1 :, :]
        middle = 0.5 * last
        fac1[q] = split_pack(jnp.exp(cum - middle))
        fac2[q] = split_pack(jnp.exp(middle - cum) * dt)
        first = (me * PER_DEV + q) * BLOCK
        on = docs(first - 1) == docs(first + BLOCK - 1)
        decay = jnp.where(jnp.broadcast_to(on, (1, 128)), jnp.exp(last), 0.0)
        packed = packed + jnp.where(rows == q, jnp.exp(middle), 0.0)
        packed = packed + jnp.where(rows == q + 4, decay, 0.0)
        packed = packed + jnp.where(rows == q + 8, through, 0.0)
        through = through * decay
    rowp[...] = split_pack(packed)
    dmine[...] = jnp.broadcast_to(through, (8, 128))
    dline[0] = dmine[...]
    for j in range(1, LINE):
        decay_copy(j).start()

    def convolved(q, where):
        window = seqx[pl.ds(pl.multiple_of(q * BLOCK, BLOCK), BLOCK + HALO), where]
        moved = jnp.dot(shifts[q], window, preferred_element_type=F32)
        weights = 0.5 * w_ref[:, where]
        half = 0.5 * b_ref[where].reshape(1, -1) + weights[3:4] * window[HALO:].astype(F32)
        for j in range(1, KW):
            half = half + weights[3 - j : 4 - j] * moved[(j - 1) * BLOCK : j * BLOCK]
        return (half + half * jnp.tanh(half)).astype(BF16)

    for o in range(4):
        exchange(chunks, o, tail_cols).wait_recv()
    place(tail_cols)
    halo(chunks, tail_cols).start()

    def projections(q, carry):
        both = convolved(q, tail_cols)
        bpart = both[:, :NS]
        cpart = both[:, NS:]
        first = (me * PER_DEV + q) * BLOCK
        row_docs = docs(iota((BLOCK, 1), 0) + first)
        scores = lax.dot_general(cpart, bpart, (((1,), (1,)), ((), ())), preferred_element_type=F32)
        keep = (row_docs == docs(iota((1, BLOCK), 1) + first)) & (col <= row)
        lhs[q, :, :BLOCK] = jnp.where(keep, scores, 0.0).astype(BF16)
        enters = row_docs == docs(first - 1)
        lhs[q, :, BLOCK:] = jnp.where(enters, cpart.astype(F32), 0.0).astype(BF16)
        stays = row_docs == docs(first + BLOCK - 1)
        btail[q] = jnp.where(stays, bpart.astype(F32), 0.0).T.astype(BF16)
        return carry

    def prepare_projections():
        halo(chunks, tail_cols).wait_recv()
        lax.fori_loop(0, PER_DEV, projections, 0)

    def prepare_decays():
        for j in range(1, LINE):
            decay_copy(j).wait_recv()
        line_rows = iota((8, 128), 0)
        line_decays = jnp.zeros((8, 128), F32)
        for n in range(LINE):
            line_decays = line_decays + jnp.where(line_rows == n, dline[lax.rem(z - n + LINE, LINE)], 0.0)
        dpack[...] = split_pack(jnp.concatenate([line_decays, jnp.zeros((8, 128), F32)], axis=0))

    def stage_arrive(k):
        for o in range(4):
            exchange(k, o, cols(k)).wait_recv()
        place(cols(k))
        halo(k, cols(k)).start()

    def stage_state(k):
        where = cols(k)
        halo(k, where).wait_recv()
        rowx[k] = jnp.dot(rowp[...], spread[:, where], preferred_element_type=F32)

        def block(q, state):
            loc[q, :, where] = state
            value = convolved(q, where)
            at_rows = pl.ds(pl.multiple_of(q * BLOCK, BLOCK), BLOCK)
            mixed[at_rows, where] = value
            factor = jnp.dot(fac2[q], spread[:, where], preferred_element_type=F32)
            scaled = (value.astype(F32) * factor).astype(BF16)
            zbuf[at_rows, where] = scaled
            added = jnp.dot(btail[q], scaled, preferred_element_type=F32)
            return rowx[k, pl.ds(q + 4, 1)] * state + rowx[k, pl.ds(q, 1)] * added

        state = jnp.zeros((NS, CHUNK), F32)
        for q in range(PER_DEV):
            state = block(q, state)
        est32[k] = state

        @pl.when(odd)
        def _():
            est[k] = state.astype(BF16)
            pair_copy(k).start()

    def stage_pair(k):
        decx[k] = jnp.dot(dpack[...], spread[:, cols(k)], preferred_element_type=F32)

        @pl.when(even)
        def _():
            pair_copy(k).wait_recv()
            est[k] = (decx[k, pl.ds(z + 1, 1)] * est32[k] + sin[k].astype(F32)).astype(BF16)
            for j in range(1, LINE):
                state_copy(k, j, pair).start()
            sbuf[k, pair] = est[k, pl.ds(pl.multiple_of(z * SLICE, SLICE), SLICE)]

    def stage_prefix(k):
        for p in range(PAIRS):
            @pl.when(z != 2 * p)
            def _(p=p):
                state_copy(k, 1, p).wait_recv()
        decays = decx[k]
        running = jnp.zeros((SLICE, CHUNK), F32)
        for p in range(PAIRS):
            runs[k, p] = running
            both = decays[2 * p : 2 * p + 1] * decays[2 * p + 1 : 2 * p + 2]
            running = both * running + sbuf[k, p].astype(F32)
        lsend[k] = running
        line_copy(k).start()

    def stage_back(k):
        line_copy(k).wait_recv()
        decays = decx[k]
        before = lrecv[k]
        for p in range(PAIRS):
            isend[k, p] = (runs[k, p] + before).astype(BF16)
            before = before * (decays[2 * p : 2 * p + 1] * decays[2 * p + 1 : 2 * p + 2])
        for p in range(PAIRS):
            @pl.when(z != 2 * p)
            def _(p=p):
                back_copy(k, p, z).start()

        @pl.when(even)
        def _():
            inc[k, pl.ds(pl.multiple_of(z * SLICE, SLICE), SLICE)] = isend[k, pair]

    def stage_relay(k):
        @pl.when(even)
        def _():
            for owner in range(LINE):
                @pl.when(z != owner)
                def _(owner=owner):
                    back_copy(k, 0, owner).wait_recv()
            rsend[k] = (decx[k, pl.ds(z, 1)] * inc[k].astype(F32) + est32[k]).astype(BF16)
            relay_copy(k).start()

    def stage_out(k):
        where = cols(k)
        @pl.when(odd)
        def _():
            relay_copy(k).wait_recv()

        entering = inc[k].astype(F32)
        for q in range(PER_DEV):
            at_rows = pl.ds(q * BLOCK, BLOCK)
            state = loc[q, :, where] + rowx[k, pl.ds(q + 8, 1)] * entering
            scaled = (rowx[k, pl.ds(q, 1)] * state).astype(BF16)
            right = jnp.concatenate([zbuf[at_rows, where], scaled], axis=0)
            value = jnp.dot(lhs[q], right, preferred_element_type=F32)
            factor = jnp.dot(fac1[q], spread[:, where], preferred_element_type=F32)
            skip = rowx[k, pl.ds(12, 1)] * mixed[at_rows, where].astype(F32)
            ybuf[at_rows, where] = (factor * value + skip).astype(BF16)
        write(k).start()

    def write(k):
        return pltpu.make_async_copy(ybuf.at[:, cols(k)], out_hbm.at[:, cols(k)], out_sem.at[k])

    def step(i, carry):
        @pl.when(i < chunks)
        def _():
            stage_arrive(i)

        pl.when(i == LAGS[0])(prepare_projections)

        @pl.when((i >= LAGS[0]) & (i - LAGS[0] < chunks))
        def _():
            stage_state(i - LAGS[0])

        pl.when(i == LAGS[1])(prepare_decays)

        @pl.when((i >= LAGS[1]) & (i - LAGS[1] < chunks))
        def _():
            stage_pair(i - LAGS[1])

        @pl.when((i >= LAGS[2]) & (i - LAGS[2] < chunks))
        def _():
            stage_prefix(i - LAGS[2])

        @pl.when((i >= LAGS[3]) & (i - LAGS[3] < chunks))
        def _():
            stage_back(i - LAGS[3])

        @pl.when((i >= LAGS[4]) & (i - LAGS[4] < chunks))
        def _():
            stage_relay(i - LAGS[4])

        @pl.when(i + AHEAD < chunks)
        def _():
            send_chunk(i + AHEAD)

        @pl.when((i >= LAGS[5]) & (i - LAGS[5] < chunks))
        def _():
            stage_out(i - LAGS[5])

        return carry

    lax.fori_loop(0, chunks + LAGS[-1], step, 0)

    for o in range(4):
        exchange_dt(o).wait_send()
        exchange(chunks, o, tail_cols).wait_send()
    halo(chunks, tail_cols).wait_send()
    for j in range(1, LINE):
        decay_copy(j).wait_send()

    def finish(k, carry):
        for o in range(4):
            exchange(k, o, cols(k)).wait_send()
        halo(k, cols(k)).wait_send()
        line_copy(k).wait_send()
        for p in range(PAIRS):
            @pl.when(z != 2 * p)
            def _(p=p):
                back_copy(k, p, z).wait_send()

        @pl.when(even)
        def _():
            for j in range(1, LINE):
                state_copy(k, j, pair).wait_send()
            relay_copy(k).wait_send()

        @pl.when(odd)
        def _():
            pair_copy(k).wait_send()

        write(k).wait()
        return carry

    lax.fori_loop(0, chunks, finish, 0)


def hand_over(source, target, held, in_sem, out_sem):
    rows = source.shape[0] // PER_DEV
    parts = [pl.ds(n * rows, rows) for n in range(PER_DEV)]
    reads = [pltpu.make_async_copy(source.at[part], held.at[part], in_sem.at[n]) for n, part in enumerate(parts)]
    writes = [pltpu.make_async_copy(held.at[part], target.at[part], out_sem.at[n]) for n, part in enumerate(parts)]
    for read in reads:
        read.start()
    for read, write in zip(reads, writes):
        read.wait()
        write.start()
    for write in writes:
        write.wait()


def body(xbc, dt_raw, conv_weight, conv_bias, dt_bias, a_log, d_skip, doc_lengths, loader_dest):
    rows, width = xbc.shape
    heads = dt_raw.shape[1]
    inner = heads * P_SIZE
    chunks = inner // CHUNK
    devices = lax.axis_size("seq")
    vmem = pl.BlockSpec(memory_space=pltpu.VMEM)
    smem = pl.BlockSpec(memory_space=pltpu.SMEM)
    anywhere = pl.BlockSpec(memory_space=pl.ANY)
    dma = pltpu.SemaphoreType.DMA
    V = pltpu.VMEM
    scratch = [
        V((PER_DEV, BLOCK, width), BF16),
        V((4, BLOCK, width), BF16),
        V((5, BLOCK, width), BF16),
        V((heads, rows), BF16),
        V((4, heads, BLOCK), BF16),
        V((5, heads, BLOCK), BF16),
        V((HALO + rows, width), BF16),
        V((rows, inner), BF16),
        V((rows, inner), BF16),
        V((PER_DEV, NS, inner), F32),
        V((chunks, NS, CHUNK), BF16),
        V((chunks, NS, CHUNK), F32),
        V((chunks, NS, CHUNK), BF16),
        V((chunks, PAIRS, SLICE, CHUNK), BF16),
        V((chunks, PAIRS, SLICE, CHUNK), F32),
        V((chunks, SLICE, CHUNK), F32),
        V((chunks, SLICE, CHUNK), F32),
        V((chunks, PAIRS, SLICE, CHUNK), BF16),
        V((chunks, NS, CHUNK), BF16),
        V((chunks, NS, CHUNK), BF16),
        V((rows, inner), BF16),
        V((128, inner), BF16),
        V((PER_DEV, (KW - 1) * BLOCK, BLOCK + HALO), BF16),
        V((PER_DEV, BLOCK, BLOCK + NS), BF16),
        V((PER_DEV, NS, BLOCK), BF16),
        V((PER_DEV, BLOCK, 128), BF16),
        V((PER_DEV, BLOCK, 128), BF16),
        V((16, 128), BF16),
        V((chunks, 16, CHUNK), F32),
        V((8, 128), F32),
        V((LINE, 8, 128), F32),
        V((16, 128), BF16),
        V((chunks, 16, CHUNK), F32),
        dma((chunks + 1,)), dma((1,)),
        dma((4, chunks + 1)), dma((4, chunks + 1)),
        dma((4,)), dma((4,)),
        dma((chunks + 1,)), dma((chunks + 1,)),
        dma((LINE,)), dma((LINE,)),
        dma((chunks, LINE)), dma((chunks, PAIRS)),
        dma((chunks,)), dma((chunks,)),
        dma((chunks, PAIRS)), dma((chunks, LINE)),
        dma((chunks,)), dma((chunks,)),
        dma((chunks,)), dma((chunks,)),
        dma((chunks,)),
    ]
    result = pl.pallas_call(
        functools.partial(kernel, devices, heads),
        out_shape=jax.ShapeDtypeStruct((rows, inner), BF16),
        in_specs=[smem, smem, anywhere, anywhere, vmem, vmem, vmem, vmem, vmem],
        out_specs=anywhere,
        scratch_shapes=scratch,
        cost_estimate=pl.CostEstimate(flops=2_000_000_000, bytes_accessed=10_000_000, transcendentals=3_000_000),
        compiler_params=pltpu.CompilerParams(
            collective_id=0, has_side_effects=True, vmem_limit_bytes=63 * 1024 * 1024),
    )(
        doc_lengths, loader_dest,
        xbc.reshape(PER_DEV, BLOCK, width), dt_raw.T,
        conv_weight, conv_bias, dt_bias[None], a_log[None], d_skip[None],
    )
    return pl.pallas_call(
        hand_over,
        out_shape=jax.ShapeDtypeStruct((rows, inner), BF16),
        in_specs=[anywhere],
        out_specs=anywhere,
        scratch_shapes=[V((rows, inner), BF16), dma((PER_DEV,)), dma((PER_DEV,))],
        compiler_params=pltpu.CompilerParams(vmem_limit_bytes=62 * 1024 * 1024),
    )(result)


def solution(mesh):
    placed = (
        P(("dp", "seq"), None),
        P(("dp", "seq"), None),
        P(),
        P(),
        P(),
        P(),
        P(),
        P("dp"),
        P("dp"),
    )
    return jax.shard_map(
        body, mesh=mesh, in_specs=placed, out_specs=P(("dp", "seq"), None), check_vma=False
    )
```

```python
import functools

import jax
import jax.numpy as jnp
from jax import lax
from jax.experimental import pallas as pl
from jax.experimental.pallas import tpu as pltpu
from jax.sharding import PartitionSpec as P

P_SIZE = 64
NS = 128
KW = 4
BLOCK = 128
PER_DEV = 4
LINE = 8
HALO = 16
CHUNK = 512
AHEAD = 2
LAGS = (1, 2, 4, 6, 8, 10)
OFFSETS = (-2, -1, 1, 2)
PAIRS = LINE // 2
SLICE = NS // PAIRS
MESH = pl.DeviceIdType.MESH
F32 = jnp.float32
BF16 = jnp.bfloat16


def iota(shape, axis):
    return lax.broadcasted_iota(jnp.int32, shape, axis)


def chosen(which, options):
    value = options[0]
    for number, option in enumerate(options[1:], 1):
        value = lax.select(which == number, option, value)
    return value


def split_pack(value):
    high = value.astype(BF16).astype(F32)
    return jnp.where(iota(value.shape, 1) < 64, high, value - high).astype(BF16)


def kernel(
    devices, heads,
    lens, dest, x_hbm, dt_hbm, w_ref, b_ref, dtb_ref, alog_ref, skip_ref,
    out_hbm,
    xin, send, recv, dtin, dtsend, dtrecv, seqx, mixed, zbuf, loc, est, est32, sin, sbuf, runs,
    lsend, lrecv, isend, rsend, inc, ybuf, spread, shifts, lhs, btail, fac1, fac2, rowp, rowx,
    dmine, dline, dpack, decx,
    in_sem, dt_sem, x_send, x_recv, d_send, d_recv, h_send, h_recv, t_send, t_recv,
    s_send, s_recv, l_send, l_recv, i_send, i_recv, p_send, p_recv, r_send, r_recv, out_sem,
):
    inner = heads * P_SIZE
    chunks = inner // CHUNK
    me = lax.axis_index("seq")
    z = lax.rem(me - lax.rem(lax.axis_index("dp"), 2) + devices, LINE)
    pair = lax.shift_right_logical(z, 1)
    even = lax.rem(z, 2) == 0
    odd = lax.rem(z, 2) == 1

    def at(offset):
        return lax.rem(me + offset + devices, devices)

    def member(place):
        return at(place - z)

    def cols(k):
        return pl.ds(pl.multiple_of(k * CHUNK, CHUNK), CHUNK)

    tail_cols = pl.ds(inner, 2 * NS)

    def load(k):
        return pltpu.make_async_copy(x_hbm.at[:, :, cols(k)], xin.at[:, :, cols(k)], in_sem.at[k])

    load_tail = pltpu.make_async_copy(x_hbm.at[:, :, tail_cols], xin.at[:, :, tail_cols], in_sem.at[chunks])
    load_dt = pltpu.make_async_copy(dt_hbm, dtin, dt_sem.at[0])
    load_dt.start()
    load_tail.start()

    def start_load(k, carry):
        load(k).start()
        return carry

    lax.fori_loop(0, chunks, start_load, 0)

    barrier = pltpu.get_barrier_semaphore()
    partners = [at(o) for o in OFFSETS] + [member(lax.rem(z + j, LINE)) for j in range(1, LINE)] + [at(LINE), at(-LINE)]
    for partner in partners:
        pl.semaphore_signal(barrier, inc=1, device_id={"seq": partner}, device_id_type=MESH)

    reach = (-2, -1, 0, 1, 2)
    own = [lax.rem(lax.shift_right_logical(dest[me * PER_DEV + j], 2) - me + 2 + devices, devices) for j in range(PER_DEV)]
    picks = []
    for number in range(5):
        pick = jnp.int32(0)
        for j in range(1, PER_DEV):
            pick = pick + jnp.where(own[j] == number, j, 0)
        picks.append(pick)
    order = {-2: 0, -1: 1, 1: 2, 2: 3, 0: 4}
    origin = [jnp.int32(0) for _ in range(PER_DEV)]
    for offset in reach:
        source = at(-offset)
        for j in range(PER_DEV):
            target = dest[source * PER_DEV + j]
            for q in range(PER_DEV):
                origin[q] = origin[q] + jnp.where(target == me * PER_DEV + q, order[offset], 0)

    def exchange(k, o, where):
        return pltpu.make_async_remote_copy(
            src_ref=send.at[o, :, where], dst_ref=recv.at[o, :, where],
            send_sem=x_send.at[o, k], recv_sem=x_recv.at[o, k],
            device_id={"seq": at(OFFSETS[o])}, device_id_type=MESH)

    def exchange_dt(o):
        return pltpu.make_async_remote_copy(
            src_ref=dtsend.at[o], dst_ref=dtrecv.at[o],
            send_sem=d_send.at[o], recv_sem=d_recv.at[o],
            device_id={"seq": at(OFFSETS[o])}, device_id_type=MESH)

    def halo(k, where):
        return pltpu.make_async_remote_copy(
            src_ref=seqx.at[pl.ds(PER_DEV * BLOCK, HALO), where], dst_ref=seqx.at[pl.ds(0, HALO), where],
            send_sem=h_send.at[k], recv_sem=h_recv.at[k],
            device_id={"seq": at(1)}, device_id_type=MESH)

    def decay_copy(j):
        return pltpu.make_async_remote_copy(
            src_ref=dmine, dst_ref=dline.at[j],
            send_sem=t_send.at[j], recv_sem=t_recv.at[j],
            device_id={"seq": member(lax.rem(z + j, LINE))}, device_id_type=MESH)

    def pair_copy(k):
        return pltpu.make_async_remote_copy(
            src_ref=est.at[k], dst_ref=sin.at[k],
            send_sem=p_send.at[k], recv_sem=p_recv.at[k],
            device_id={"seq": at(-1)}, device_id_type=MESH)

    def relay_copy(k):
        return pltpu.make_async_remote_copy(
            src_ref=rsend.at[k], dst_ref=inc.at[k],
            send_sem=r_send.at[k], recv_sem=r_recv.at[k],
            device_id={"seq": at(1)}, device_id_type=MESH)

    def state_copy(k, j, sender):
        target = lax.rem(pair + j, PAIRS)
        return pltpu.make_async_remote_copy(
            src_ref=est.at[k, pl.ds(pl.multiple_of(target * SLICE, SLICE), SLICE)], dst_ref=sbuf.at[k, sender],
            send_sem=s_send.at[k, j], recv_sem=s_recv.at[k, sender],
            device_id={"seq": member(2 * target)}, device_id_type=MESH)

    def line_copy(k):
        return pltpu.make_async_remote_copy(
            src_ref=lsend.at[k], dst_ref=lrecv.at[k],
            send_sem=l_send.at[k], recv_sem=l_recv.at[k],
            device_id={"seq": at(LINE)}, device_id_type=MESH)

    def back_copy(k, p, sender):
        return pltpu.make_async_remote_copy(
            src_ref=isend.at[k, p], dst_ref=inc.at[k, pl.ds(pl.multiple_of(sender * SLICE, SLICE), SLICE)],
            send_sem=i_send.at[k, p], recv_sem=i_recv.at[k, sender],
            device_id={"seq": member(2 * p)}, device_id_type=MESH)

    def fill(where):
        blocks = [xin[j, :, where] for j in range(PER_DEV)]
        for o, offset in enumerate(OFFSETS):
            send[o, :, where] = chosen(picks[offset + 2], blocks)
        recv[4, :, where] = chosen(picks[2], blocks)

    def place(where):
        options = [recv[o, :, where] for o in range(5)]
        for q in range(PER_DEV):
            seqx[pl.ds(HALO + q * BLOCK, BLOCK), where] = chosen(origin[q], options)

    def send_chunk(k):
        load(k).wait()
        fill(cols(k))
        for o in range(4):
            exchange(k, o, cols(k)).start()

    load_dt.wait()
    dt_blocks = [dtin[:, j * BLOCK : (j + 1) * BLOCK] for j in range(PER_DEV)]
    for o, offset in enumerate(OFFSETS):
        dtsend[o] = chosen(picks[offset + 2], dt_blocks)
    dtrecv[4] = chosen(picks[2], dt_blocks)
    load_tail.wait()
    fill(tail_cols)
    pl.semaphore_wait(barrier, len(partners))
    for o in range(4):
        exchange_dt(o).start()
        exchange(chunks, o, tail_cols).start()
    for k in range(AHEAD):
        send_chunk(k)

    starts = []
    total = jnp.int32(0)
    for n in range(lens.shape[0]):
        starts.append(total)
        total = total + lens[n]

    def docs(positions):
        found = jnp.where(starts[0] <= positions, 0, -1)
        for begin in starts[1:]:
            found = found + jnp.where(begin <= positions, 1, 0)
        return found

    row = iota((BLOCK, BLOCK), 0)
    col = iota((BLOCK, BLOCK), 1)
    square = (BLOCK, BLOCK + HALO)

    def make_shift(q, carry):
        first = (me * PER_DEV + q) * BLOCK
        same = docs(iota((BLOCK, 1), 0) + first) == docs(iota((1, BLOCK + HALO), 1) + (first - HALO))
        apart = iota(square, 1) - iota(square, 0)
        for j in range(1, KW):
            keep = same & (apart == HALO - j)
            shifts[q, pl.ds((j - 1) * BLOCK, BLOCK), :] = jnp.where(keep, 1.0, 0.0).astype(BF16)
        return carry

    lax.fori_loop(0, PER_DEV, make_shift, 0)

    def make_spread(k, carry):
        head = lax.shift_right_logical(iota((128, CHUNK), 1) + k * CHUNK, 6)
        match = (iota((128, CHUNK), 0) & 63) == head
        spread[:, cols(k)] = jnp.where(match, 1.0, 0.0).astype(BF16)
        return carry

    lax.fori_loop(0, chunks, make_spread, 0)

    double = jnp.where((iota((heads, 128), 1) & 63) == iota((heads, 128), 0), 1.0, 0.0)
    which = iota((8, heads), 0)
    stacked = jnp.where(which == 0, dtb_ref[...], jnp.where(which == 1, alog_ref[...], skip_ref[...]))
    params = jnp.dot(stacked, double, precision=lax.Precision.HIGHEST, preferred_element_type=F32)
    lower = jnp.where(col <= row, 1.0, 0.0)

    for o in range(4):
        exchange_dt(o).wait_recv()
    through = jnp.ones((1, 128), F32)
    dt_options = [dtrecv[o] for o in range(5)]
    rows = iota((16, 128), 0)
    packed = jnp.where(rows == 12, params[2:3], 0.0)
    for q in range(PER_DEV):
        raw = lax.dot_general(
            chosen(origin[q], dt_options), double.astype(BF16), (((0,), (0,)), ((), ())),
            preferred_element_type=F32) + params[0:1]
        dt = jnp.maximum(raw, 0.0) + jnp.log1p(jnp.exp(-jnp.abs(raw)))
        rate = -jnp.exp(params[1:2]) * dt
        cum = jnp.dot(lower, rate, precision=lax.Precision.HIGHEST, preferred_element_type=F32)
        last = cum[BLOCK - 1 :, :]
        middle = 0.5 * last
        fac1[q] = split_pack(jnp.exp(cum - middle))
        fac2[q] = split_pack(jnp.exp(middle - cum) * dt)
        first = (me * PER_DEV + q) * BLOCK
        on = docs(first - 1) == docs(first + BLOCK - 1)
        decay = jnp.where(jnp.broadcast_to(on, (1, 128)), jnp.exp(last), 0.0)
        packed = packed + jnp.where(rows == q, jnp.exp(middle), 0.0)
        packed = packed + jnp.where(rows == q + 4, decay, 0.0)
        packed = packed + jnp.where(rows == q + 8, through, 0.0)
        through = through * decay
    rowp[...] = split_pack(packed)
    dmine[...] = jnp.broadcast_to(through, (8, 128))
    dline[0] = dmine[...]
    for j in range(1, LINE):
        decay_copy(j).start()

    def convolved(q, where):
        window = seqx[pl.ds(pl.multiple_of(q * BLOCK, BLOCK), BLOCK + HALO), where]
        moved = jnp.dot(shifts[q], window, preferred_element_type=F32)
        weights = 0.5 * w_ref[:, where]
        half = 0.5 * b_ref[where].reshape(1, -1) + weights[3:4] * window[HALO:].astype(F32)
        for j in range(1, KW):
            half = half + weights[3 - j : 4 - j] * moved[(j - 1) * BLOCK : j * BLOCK]
        return (half + half * jnp.tanh(half)).astype(BF16)

    for o in range(4):
        exchange(chunks, o, tail_cols).wait_recv()
    place(tail_cols)
    halo(chunks, tail_cols).start()

    def projections(q, carry):
        both = convolved(q, tail_cols)
        bpart = both[:, :NS]
        cpart = both[:, NS:]
        first = (me * PER_DEV + q) * BLOCK
        row_docs = docs(iota((BLOCK, 1), 0) + first)
        scores = lax.dot_general(cpart, bpart, (((1,), (1,)), ((), ())), preferred_element_type=F32)
        keep = (row_docs == docs(iota((1, BLOCK), 1) + first)) & (col <= row)
        lhs[q, :, :BLOCK] = jnp.where(keep, scores, 0.0).astype(BF16)
        enters = row_docs == docs(first - 1)
        lhs[q, :, BLOCK:] = jnp.where(enters, cpart.astype(F32), 0.0).astype(BF16)
        stays = row_docs == docs(first + BLOCK - 1)
        btail[q] = jnp.where(stays, bpart.astype(F32), 0.0).T.astype(BF16)
        return carry

    def prepare_projections():
        halo(chunks, tail_cols).wait_recv()
        lax.fori_loop(0, PER_DEV, projections, 0)

    def prepare_decays():
        for j in range(1, LINE):
            decay_copy(j).wait_recv()
        line_rows = iota((8, 128), 0)
        line_decays = jnp.zeros((8, 128), F32)
        for n in range(LINE):
            line_decays = line_decays + jnp.where(line_rows == n, dline[lax.rem(z - n + LINE, LINE)], 0.0)
        dpack[...] = split_pack(jnp.concatenate([line_decays, jnp.zeros((8, 128), F32)], axis=0))

    def stage_arrive(k):
        for o in range(4):
            exchange(k, o, cols(k)).wait_recv()
        place(cols(k))
        halo(k, cols(k)).start()

    def stage_state(k):
        where = cols(k)
        halo(k, where).wait_recv()
        rowx[k] = jnp.dot(rowp[...], spread[:, where], preferred_element_type=F32)

        def block(q, state):
            loc[q, :, where] = state
            value = convolved(q, where)
            at_rows = pl.ds(pl.multiple_of(q * BLOCK, BLOCK), BLOCK)
            mixed[at_rows, where] = value
            factor = jnp.dot(fac2[q], spread[:, where], preferred_element_type=F32)
            scaled = (value.astype(F32) * factor).astype(BF16)
            zbuf[at_rows, where] = scaled
            added = jnp.dot(btail[q], scaled, preferred_element_type=F32)
            return rowx[k, pl.ds(q + 4, 1)] * state + rowx[k, pl.ds(q, 1)] * added

        state = jnp.zeros((NS, CHUNK), F32)
        for q in range(PER_DEV):
            state = block(q, state)
        est32[k] = state

        @pl.when(odd)
        def _():
            est[k] = state.astype(BF16)
            pair_copy(k).start()

    def stage_pair(k):
        decx[k] = jnp.dot(dpack[...], spread[:, cols(k)], preferred_element_type=F32)

        @pl.when(even)
        def _():
            pair_copy(k).wait_recv()
            est[k] = (decx[k, pl.ds(z + 1, 1)] * est32[k] + sin[k].astype(F32)).astype(BF16)
            for j in range(1, PAIRS):
                state_copy(k, j, pair).start()
            sbuf[k, pair] = est[k, pl.ds(pl.multiple_of(pair * SLICE, SLICE), SLICE)]

    def stage_prefix(k):
        for p in range(PAIRS):
            @pl.when(pair != p)
            def _(p=p):
                state_copy(k, 1, p).wait_recv()
        decays = decx[k]
        running = jnp.zeros((SLICE, CHUNK), F32)
        for p in range(PAIRS):
            runs[k, p] = running
            both = decays[2 * p : 2 * p + 1] * decays[2 * p + 1 : 2 * p + 2]
            running = both * running + sbuf[k, p].astype(F32)
        lsend[k] = running
        line_copy(k).start()

    def stage_back(k):
        line_copy(k).wait_recv()
        decays = decx[k]
        before = lrecv[k]
        for p in range(PAIRS):
            isend[k, p] = (runs[k, p] + before).astype(BF16)
            before = before * (decays[2 * p : 2 * p + 1] * decays[2 * p + 1 : 2 * p + 2])
        for p in range(PAIRS):
            @pl.when(pair != p)
            def _(p=p):
                back_copy(k, p, pair).start()

        inc[k, pl.ds(pl.multiple_of(pair * SLICE, SLICE), SLICE)] = isend[k, pair]

    def stage_relay(k):
        @pl.when(even)
        def _():
            for owner in range(PAIRS):
                @pl.when(pair != owner)
                def _(owner=owner):
                    back_copy(k, 0, owner).wait_recv()
            rsend[k] = (decx[k, pl.ds(z, 1)] * inc[k].astype(F32) + est32[k]).astype(BF16)
            relay_copy(k).start()

    def stage_out(k):
        where = cols(k)
        @pl.when(odd)
        def _():
            relay_copy(k).wait_recv()

        entering = inc[k].astype(F32)
        for q in range(PER_DEV):
            at_rows = pl.ds(q * BLOCK, BLOCK)
            state = loc[q, :, where] + rowx[k, pl.ds(q + 8, 1)] * entering
            scaled = (rowx[k, pl.ds(q, 1)] * state).astype(BF16)
            right = jnp.concatenate([zbuf[at_rows, where], scaled], axis=0)
            value = jnp.dot(lhs[q], right, preferred_element_type=F32)
            factor = jnp.dot(fac1[q], spread[:, where], preferred_element_type=F32)
            skip = rowx[k, pl.ds(12, 1)] * mixed[at_rows, where].astype(F32)
            ybuf[at_rows, where] = (factor * value + skip).astype(BF16)
        write(k).start()

    def write(k):
        return pltpu.make_async_copy(ybuf.at[:, cols(k)], out_hbm.at[:, cols(k)], out_sem.at[k])

    def step(i, carry):
        @pl.when(i < chunks)
        def _():
            stage_arrive(i)

        pl.when(i == LAGS[0])(prepare_projections)

        @pl.when((i >= LAGS[0]) & (i - LAGS[0] < chunks))
        def _():
            stage_state(i - LAGS[0])

        pl.when(i == LAGS[1])(prepare_decays)

        @pl.when((i >= LAGS[1]) & (i - LAGS[1] < chunks))
        def _():
            stage_pair(i - LAGS[1])

        @pl.when(even & (i >= LAGS[2]) & (i - LAGS[2] < chunks))
        def _():
            stage_prefix(i - LAGS[2])

        @pl.when(even & (i >= LAGS[3]) & (i - LAGS[3] < chunks))
        def _():
            stage_back(i - LAGS[3])

        @pl.when((i >= LAGS[4]) & (i - LAGS[4] < chunks))
        def _():
            stage_relay(i - LAGS[4])

        @pl.when(i + AHEAD < chunks)
        def _():
            send_chunk(i + AHEAD)

        @pl.when((i >= LAGS[5]) & (i - LAGS[5] < chunks))
        def _():
            stage_out(i - LAGS[5])

        return carry

    lax.fori_loop(0, chunks + LAGS[-1], step, 0)

    for o in range(4):
        exchange_dt(o).wait_send()
        exchange(chunks, o, tail_cols).wait_send()
    halo(chunks, tail_cols).wait_send()
    for j in range(1, LINE):
        decay_copy(j).wait_send()

    def finish(k, carry):
        for o in range(4):
            exchange(k, o, cols(k)).wait_send()
        halo(k, cols(k)).wait_send()
        for p in range(PAIRS):
            @pl.when(even & (pair != p))
            def _(p=p):
                back_copy(k, p, pair).wait_send()

        @pl.when(even)
        def _():
            for j in range(1, PAIRS):
                state_copy(k, j, pair).wait_send()
            relay_copy(k).wait_send()
            line_copy(k).wait_send()

        @pl.when(odd)
        def _():
            pair_copy(k).wait_send()

        write(k).wait()
        return carry

    lax.fori_loop(0, chunks, finish, 0)


def hand_over(source, target, held, in_sem, out_sem):
    rows = source.shape[0] // PER_DEV
    parts = [pl.ds(n * rows, rows) for n in range(PER_DEV)]
    reads = [pltpu.make_async_copy(source.at[part], held.at[part], in_sem.at[n]) for n, part in enumerate(parts)]
    writes = [pltpu.make_async_copy(held.at[part], target.at[part], out_sem.at[n]) for n, part in enumerate(parts)]
    for read in reads:
        read.start()
    for read, write in zip(reads, writes):
        read.wait()
        write.start()
    for write in writes:
        write.wait()


def body(xbc, dt_raw, conv_weight, conv_bias, dt_bias, a_log, d_skip, doc_lengths, loader_dest):
    rows, width = xbc.shape
    heads = dt_raw.shape[1]
    inner = heads * P_SIZE
    chunks = inner // CHUNK
    devices = lax.axis_size("seq")
    vmem = pl.BlockSpec(memory_space=pltpu.VMEM)
    smem = pl.BlockSpec(memory_space=pltpu.SMEM)
    anywhere = pl.BlockSpec(memory_space=pl.ANY)
    dma = pltpu.SemaphoreType.DMA
    V = pltpu.VMEM
    scratch = [
        V((PER_DEV, BLOCK, width), BF16),
        V((4, BLOCK, width), BF16),
        V((5, BLOCK, width), BF16),
        V((heads, rows), BF16),
        V((4, heads, BLOCK), BF16),
        V((5, heads, BLOCK), BF16),
        V((HALO + rows, width), BF16),
        V((rows, inner), BF16),
        V((rows, inner), BF16),
        V((PER_DEV, NS, inner), F32),
        V((chunks, NS, CHUNK), BF16),
        V((chunks, NS, CHUNK), F32),
        V((chunks, NS, CHUNK), BF16),
        V((chunks, PAIRS, SLICE, CHUNK), BF16),
        V((chunks, PAIRS, SLICE, CHUNK), F32),
        V((chunks, SLICE, CHUNK), F32),
        V((chunks, SLICE, CHUNK), F32),
        V((chunks, PAIRS, SLICE, CHUNK), BF16),
        V((chunks, NS, CHUNK), BF16),
        V((chunks, NS, CHUNK), BF16),
        V((rows, inner), BF16),
        V((128, inner), BF16),
        V((PER_DEV, (KW - 1) * BLOCK, BLOCK + HALO), BF16),
        V((PER_DEV, BLOCK, BLOCK + NS), BF16),
        V((PER_DEV, NS, BLOCK), BF16),
        V((PER_DEV, BLOCK, 128), BF16),
        V((PER_DEV, BLOCK, 128), BF16),
        V((16, 128), BF16),
        V((chunks, 16, CHUNK), F32),
        V((8, 128), F32),
        V((LINE, 8, 128), F32),
        V((16, 128), BF16),
        V((chunks, 16, CHUNK), F32),
        dma((chunks + 1,)), dma((1,)),
        dma((4, chunks + 1)), dma((4, chunks + 1)),
        dma((4,)), dma((4,)),
        dma((chunks + 1,)), dma((chunks + 1,)),
        dma((LINE,)), dma((LINE,)),
        dma((chunks, LINE)), dma((chunks, PAIRS)),
        dma((chunks,)), dma((chunks,)),
        dma((chunks, PAIRS)), dma((chunks, LINE)),
        dma((chunks,)), dma((chunks,)),
        dma((chunks,)), dma((chunks,)),
        dma((chunks,)),
    ]
    result = pl.pallas_call(
        functools.partial(kernel, devices, heads),
        out_shape=jax.ShapeDtypeStruct((rows, inner), BF16),
        in_specs=[smem, smem, anywhere, anywhere, vmem, vmem, vmem, vmem, vmem],
        out_specs=anywhere,
        scratch_shapes=scratch,
        cost_estimate=pl.CostEstimate(flops=2_000_000_000, bytes_accessed=10_000_000, transcendentals=3_000_000),
        compiler_params=pltpu.CompilerParams(
            collective_id=0, has_side_effects=True, vmem_limit_bytes=63 * 1024 * 1024),
    )(
        doc_lengths, loader_dest,
        xbc.reshape(PER_DEV, BLOCK, width), dt_raw.T,
        conv_weight, conv_bias, dt_bias[None], a_log[None], d_skip[None],
    )
    return pl.pallas_call(
        hand_over,
        out_shape=jax.ShapeDtypeStruct((rows, inner), BF16),
        in_specs=[anywhere],
        out_specs=anywhere,
        scratch_shapes=[V((rows, inner), BF16), dma((PER_DEV,)), dma((PER_DEV,))],
        compiler_params=pltpu.CompilerParams(vmem_limit_bytes=62 * 1024 * 1024),
    )(result)


def solution(mesh):
    placed = (
        P(("dp", "seq"), None),
        P(("dp", "seq"), None),
        P(),
        P(),
        P(),
        P(),
        P(),
        P("dp"),
        P("dp"),
    )
    return jax.shard_map(
        body, mesh=mesh, in_specs=placed, out_specs=P(("dp", "seq"), None), check_vma=False
    )
```
